256 devices in a mesh: ctx: 32 (over z, x), head: 8 (over y, core).
Axes of the slice: x: 4, y: 4, z: 8, core: 2. Of those that a mesh axis runs over, the one named last changes fastest.
Arguments:
- q_nope: bfloat16 [4096, 8192], P('ctx', 'head'), may hold values from -6 to 6
- q_rope: bfloat16 [4096, 4096], P('ctx', 'head'), may hold values from -300 to 300
- latent: bfloat16 [4096, 512], P('ctx'), may hold values from -6 to 6
- k_rope: bfloat16 [4096, 64], P('ctx'), may hold values from -4 to 4
- span_order: int32 [64], replicated, may hold values from 0 to 63, each once
- w_uk: bfloat16 [512, 8192], P(None, 'head'), may hold values from -0.25 to 0.25
- w_uv: bfloat16 [512, 8192], P(None, 'head'), may hold values from -0.25 to 0.25
- w_o: bfloat16 [8192, 7168], P('head', 'ctx'), may hold values from -0.125 to 0.125
Outputs:
- attended: bfloat16 [4096, 7168], P('ctx', 'head')
The draws below stay inside these ranges and needn't reach their ends.
Inputs may be any that keep to these rules, and one draw needn't show every extreme that they name: `span_order`: a permutation of 0 to 63.
All inputs are finite; a program needn't handle non-finite values.
Results may differ from the reference program's by a relative error of at most 0.014.
Values may be sent and summed in bfloat16 or wider, within the bound.
A program may use at most 128 MiB of HBM per device.

```python
import math
import jax
import jax.numpy as jnp
from jax import lax

D = 7168
LAT = 512
ROPE = 64
NOPE = 128
VDIM = 128
HEAD_DEV = 8
TOK_DEV = 128
HEADS = 64
TOKENS = 4096
SPANS = 64
N_HEAD = 8


def rope_pair(key):
    keys_rot = jnp.clip(jax.random.normal(jax.random.fold_in(key, 11), (TOKENS, ROPE), jnp.float32), -4.0, 4.0)
    query_rot = jnp.clip(jax.random.normal(jax.random.fold_in(key, 12), (TOKENS, HEADS * ROPE), jnp.float32), -4.0, 4.0)
    return (query_rot, keys_rot)


def draw_q_rope(key, part):
    return rope_pair(key)[0].astype(jnp.bfloat16)


def draw_k_rope(key, part):
    return rope_pair(key)[1].astype(jnp.bfloat16)


def raised(entries, stream_key, source, target, blocks, factor):
    def block_of(dim):
        return (jnp.arange(entries.shape[dim]) // (entries.shape[dim] // blocks)).reshape((-1,) + (1,) * (entries.ndim - 1 - dim))

    near = jax.random.permutation(stream_key, blocks)[block_of(target)]
    far = (block_of(target) + blocks // 2) % blocks
    return jnp.where((block_of(source) == near) | (block_of(source) == far), factor * entries, entries)


def steps_of(own_key, shape, cuts, low, largest):
    def one(position, parts):
        heights = jax.random.uniform(jax.random.fold_in(jax.random.fold_in(own_key, 6), position), (parts,), jnp.float32, low / len(cuts), largest / len(cuts))
        return jnp.repeat(jnp.exp(heights), shape[position] // parts).reshape((-1,) + (1,) * (len(shape) - position - 1))

    gain = one(*cuts[0])
    for cut in cuts[1:]:
        gain = gain * one(*cut)
    return gain


def scatter_about(key, extent, spread, limit, cuts=(), kind=jnp.bfloat16):
    gain = steps_of(key, extent, cuts, -0.22, 0.18) if cuts else 1.0
    result = jax.random.normal(key, extent, jnp.float32) * spread * gain
    return jnp.minimum(jnp.maximum(result, -limit), limit).astype(kind)


def noise_with(rng, dims, scale, most, shards, heavy, held_as=jnp.bfloat16):
    array = scale * jax.random.normal(rng, dims, jnp.float32)
    if shards:
        array = array * steps_of(rng, dims, shards, -0.22, 0.18)
    return jnp.clip(raised(array, jax.random.fold_in(rng, 3), *heavy), -most, most).astype(held_as)


def setup_inputs(seed: int = 0) -> dict:
    key_list = jax.random.split(jax.random.key(seed), 9)
    return {
        "q_nope": scatter_about(key_list[0], (TOKENS, HEADS * NOPE), 1.0, 6.0, ((0, 32), (1, 8))),
        "q_rope": draw_q_rope(jax.random.fold_in(key_list[8], 71), 0),
        "latent": scatter_about(key_list[2], (TOKENS, LAT), 1.0, 6.0, ((0, 32),)),
        "k_rope": draw_k_rope(jax.random.fold_in(key_list[8], 71), 0),
        "span_order": jax.random.permutation(key_list[4], SPANS).astype(jnp.int32),
        "w_uk": scatter_about(key_list[5], (LAT, HEADS * NOPE), LAT ** -0.5, 0.25, ((1, 8),)),
        "w_uv": scatter_about(key_list[6], (LAT, HEADS * VDIM), LAT ** -0.5, 0.25, ((1, 8),)),
        "w_o": noise_with(key_list[7], (HEADS * VDIM, D), (HEADS * VDIM) ** -0.5, 0.125, ((0, 8), (1, 32)), (0, 1, 32, 2.75)),
    }


def reference(q_nope, q_rope, latent, k_rope, span_order, w_uk, w_uv, w_o):
    half = TOK_DEV // 2
    heads = HEADS
    scale = 1.0 / math.sqrt(NOPE + ROPE)
    slot_ids = jnp.arange(SPANS, dtype=jnp.int32)
    slot_of_span = jnp.zeros((SPANS,), jnp.int32).at[span_order].set(slot_ids)
    places = jnp.arange(TOKENS, dtype=jnp.int32)
    row_of = (slot_of_span[places // half] * half + places % half).astype(jnp.int32)
    qn = q_nope[row_of].reshape(TOKENS, heads, NOPE)
    qr = q_rope[row_of].reshape(TOKENS, heads, ROPE)
    lat = latent[row_of]
    kr = k_rope[row_of]
    up_key = w_uk.reshape(LAT, heads, NOPE).astype(jnp.float32)
    up_value = w_uv.reshape(LAT, heads, VDIM).astype(jnp.float32)
    lat_f = lat.astype(jnp.float32)
    kr_f = kr.astype(jnp.float32)
    group_rows = HEAD_DEV * VDIM
    block = math.gcd(TOKENS, 512)
    pieces = []
    for index in range(TOKENS // block):
        low = index * block
        high = low + block
        absorbed = jnp.einsum('thn,lhn->htl', qn[low:high].astype(jnp.float32), up_key).astype(jnp.bfloat16)
        score = jnp.einsum('htl,kl->htk', absorbed.astype(jnp.float32), lat_f[:high])
        score = score + jnp.einsum('thr,kr->htk', qr[low:high].astype(jnp.float32), kr_f[:high])
        score = score * scale
        qpos = jnp.arange(low, high, dtype=jnp.int32)
        kpos = jnp.arange(0, high, dtype=jnp.int32)
        visible = kpos[None, None, :] <= qpos[None, :, None]
        top = lax.optimization_barrier(jnp.max(jnp.where(visible, score, -1e+30), axis=-1))
        weight = jnp.where(visible, jnp.exp(score - top[..., None]), 0.0)
        total = lax.optimization_barrier(jnp.sum(weight, axis=-1))
        weight_bf = weight.astype(jnp.bfloat16)
        context = jnp.einsum('htk,kl->htl', weight_bf.astype(jnp.float32), lat_f[:high])
        context = (context / total[..., None]).astype(jnp.bfloat16)
        heads_out = jnp.einsum('htl,lhv->thv', context.astype(jnp.float32), up_value).astype(jnp.bfloat16)
        heads_out = heads_out.reshape(block, heads * VDIM)
        summed = jnp.zeros((block, D), jnp.float32)
        for group in range(N_HEAD):
            first = group * group_rows
            part = jnp.dot(heads_out[:, first:first + group_rows], w_o[first:first + group_rows], preferred_element_type=jnp.float32).astype(jnp.bfloat16)
            summed = summed + part.astype(jnp.float32)
        pieces.append(summed.astype(jnp.bfloat16))
    ordered = jnp.concatenate(pieces, axis=0)
    rows = jnp.arange(TOKENS, dtype=jnp.int32)
    place_of_row = (span_order[rows // half] * half + rows % half).astype(jnp.int32)
    return ordered[place_of_row]
```

```python
import functools
import math

import jax
import jax.numpy as jnp
from jax import lax
from jax.experimental import pallas as pl
from jax.experimental.pallas import tpu as pltpu
from jax.sharding import Mesh
from jax.sharding import PartitionSpec as P

NZ, NX, NY = 8, 4, 4
TOK, SPAN = 128, 64
HEADS, NOPE, ROPE, LAT, VDIM = 8, 128, 64, 512, 128
WIDE = LAT + 2 * ROPE
COLS = 224
PAIRS = HEADS // 2
KEYS = NZ * NX * TOK
CHUNK = 512
FACTOR = math.log2(math.e) / math.sqrt(NOPE + ROPE)
HIDDEN = -1e30
MESH = pl.DeviceIdType.MESH
DELTAS = (0, -1, 1, -2, 2, -3, 3, -4)


def nt_dot(a, b):
    return lax.dot_general(a, b, (((1,), (1,)), ((), ())), preferred_element_type=jnp.float32)


def nn_dot(a, b):
    return jnp.dot(a, b, preferred_element_type=jnp.float32)


def kernel(
    qn, qr, lat, kr, order, wuk, wuv, wo, out,
    kbuf, stage, own_rope, qaug, acc, wbuf, hog, c1s, c1r, c2s, c2r, c3s, c3r,
    shift_sem, z_sem, w_sem, p_sem, o_sem, a_sem, c1_sem, c2_sem, c3_sem,
):
    z, x, y, core = (lax.axis_index(n) for n in ("z", "x", "y", "core"))
    other = 1 - core

    def at(dz=0, dx=0, dy=0):
        return (lax.rem(z + NZ + dz, NZ), lax.rem(x + NX + dx, NX), lax.rem(y + NY + dy, NY), core)

    partner = (z, x, y, other)
    peers = [at(dz=1), at(dz=-1), partner]
    peers += [at(dx=d) for d in (1, 2, 3)] + [at(dy=d) for d in (1, 2, 3)]
    barrier = pltpu.get_barrier_semaphore()
    for peer in peers:
        pl.semaphore_signal(barrier, inc=1, device_id=peer, device_id_type=MESH)

    sent = []

    def copy(src, dst, sems, device):
        return pltpu.make_async_remote_copy(
            src_ref=src, dst_ref=dst, send_sem=sems[0], recv_sem=sems[1], device_id=device, device_id_type=MESH
        )

    def send(src, dst, sems, device):
        made = copy(src, dst, sems, device)
        made.start()
        sent.append(made)

    def arrived(dst, sems, device):
        copy(dst, dst, sems, device).wait_recv()

    def pair_of(sems, *index):
        return sems.at[(0, *index)], sems.at[(1, *index)]

    own_slot = (z * NX + x) * 2 + core
    lane = lax.broadcasted_iota(jnp.int32, (SPAN, 2 * ROPE), 1)
    own_rope[...] = jnp.zeros_like(own_rope)
    own_rope[:, :ROPE] = kr[...]
    mine = pl.ds(pl.multiple_of(core * SPAN, SPAN), SPAN)
    stage[:, :LAT] = lat[mine, :]
    stage[:, LAT:] = jnp.where(
        lane == ROPE + own_slot, 1.0, own_rope[mine, :].astype(jnp.float32)
    ).astype(jnp.bfloat16)

    pl.semaphore_wait(barrier, len(peers))

    def sigma(k):
        return 1 - 2 * k

    def piece(k, delta, off):
        zz = lax.rem(z + NZ + sigma(k) * delta, NZ)
        xx = lax.rem(x + y * k + off + NX, NX)
        start = ((zz * NX + xx) * 2 + k) * SPAN
        return kbuf.at[pl.ds(pl.multiple_of(start, SPAN), SPAN)]

    def wdev(step):
        return at(dx=other * step, dy=core * step)

    zdev = {True: at(dz=sigma(core)), False: at(dz=-sigma(core))}
    own_rows = pl.ds(pl.multiple_of(own_slot * SPAN, SPAN), SPAN)
    shift_dev = at(dx=-(core * y))
    shift = copy(stage, kbuf.at[own_rows], (shift_sem.at[0], shift_sem.at[1]), shift_dev)

    @pl.when(core * y == 0)
    def _():
        kbuf[own_rows, :] = stage[...]

    @pl.when(core * y != 0)
    def _():
        shift.start()
        arrived(piece(core, 0, 0), (shift_sem.at[0], shift_sem.at[1]), shift_dev)

    def spread(i, delta):
        here = piece(core, delta, 0)
        for step, side in ((1, 0), (-1, 1)):
            send(here, here, pair_of(w_sem, side, i), wdev(step))
        send(here, here, pair_of(p_sem, 0, i), partner)

    for i, delta in enumerate(DELTAS):
        here = piece(core, delta, 0)
        if i:
            arrived(here, pair_of(z_sem, i), zdev[delta > 0])
        for later in range(i + 1, NZ):
            if (i == 0 and later < 3) or (i > 0 and later == i + 2):
                send(here, here, pair_of(z_sem, later), zdev[DELTAS[later] < 0])
        spread(i, delta)

    def wpart(delta, half):
        zz = lax.rem(z + NZ + sigma(core) * delta, NZ)
        return wbuf.at[zz, pl.ds(half * 512, 512)]

    for half in range(2):
        for later in (1, 2):
            send(wo.at[pl.ds(half * 512, 512)], wpart(0, half), pair_of(o_sem, half, later), zdev[DELTAS[later] < 0])
    wbuf[z] = wo[...]

    def serve_w(i):
        for half in range(2):
            here = wpart(DELTAS[i], half)
            arrived(here, pair_of(o_sem, half, i), zdev[DELTAS[i] > 0])
            if i + 2 < NZ:
                send(here, here, pair_of(o_sem, half, i + 2), zdev[DELTAS[i + 2] < 0])

    wide_lane = lax.broadcasted_iota(jnp.int32, (1, 2 * ROPE), 1)
    places = jnp.concatenate([order[...], order[...]], axis=1)
    half_of = lax.broadcasted_iota(jnp.int32, (TOK, 2 * ROPE), 0) // SPAN
    hidden = []
    for half in range(2):
        slot = (z * NX + x) * 2 + half
        place = jnp.sum(jnp.where(wide_lane == slot, places, 0), axis=1, keepdims=True)
        hidden.append(jnp.where(places >= place, HIDDEN, 0.0))
    mask = jnp.where(half_of == 0, hidden[0], hidden[1])
    low = lax.broadcasted_iota(jnp.int32, (TOK, 2 * ROPE), 1) < ROPE
    for h in range(HEADS):
        rows = pl.ds((h % 2) * TOK, TOK)
        cols = pl.ds(h * NOPE, NOPE)
        qaug[h // 2, rows, :LAT] = nt_dot(qn[:, cols], wuk[:, cols]).astype(jnp.bfloat16)
        rot = qr[:, pl.ds((h // 2) * 2 * ROPE, 2 * ROPE)].astype(jnp.float32)
        if h % 2:
            rot = pltpu.roll(rot, ROPE, 1)
        qaug[h // 2, rows, LAT:] = jnp.where(low, rot, mask).astype(jnp.bfloat16)

    for i, delta in enumerate(DELTAS):
        left, right = piece(core, delta, -1), piece(core, delta, 1)
        arrived(left, pair_of(w_sem, 0, i), wdev(-1))
        arrived(right, pair_of(w_sem, 1, i), wdev(1))
        parity = lax.rem(z + NZ + delta, 2)
        onward = piece(core, delta, 2 * parity - 1)
        send(onward, onward, pair_of(w_sem, 2, i), wdev(1 - 2 * parity))
        send(left, left, pair_of(p_sem, 1, i), partner)
        send(right, right, pair_of(p_sem, 2, i), partner)
    for i, delta in enumerate(DELTAS):
        far = piece(core, delta, 2)
        arrived(far, pair_of(w_sem, 2, i), wdev(1))
        send(far, far, pair_of(p_sem, 3, i), partner)
    for n, off in enumerate((0, -1, 1, 2)):
        for i, delta in enumerate(DELTAS):
            arrived(piece(other, delta, off), pair_of(p_sem, n, i), partner)

    row = lax.rem(lax.broadcasted_iota(jnp.int32, (2 * TOK, TOK), 0), TOK)
    col = lax.broadcasted_iota(jnp.int32, (2 * TOK, TOK), 1)
    seen = (col <= row) & (col >= (row // SPAN) * SPAN)

    for g in range(PAIRS):
        first = nt_dot(qaug[g, :, :LAT], lat[...]) + nt_dot(qaug[g, :, LAT:], own_rope[...])
        first = jnp.where(seen, first * FACTOR, HIDDEN)
        top = jnp.max(first, axis=1, keepdims=True)
        weight = jnp.exp2(first - top)
        total = jnp.sum(weight, axis=1, keepdims=True)
        acc[...] = nn_dot(weight.astype(jnp.bfloat16), lat[...])

        def body(n, carry):
            top, total = carry
            spots = [pl.ds(pl.multiple_of((2 * n + k) * CHUNK, CHUNK), CHUNK) for k in range(2)]
            scores = [nt_dot(qaug[g], kbuf[spot, :]) * FACTOR for spot in spots]
            for spot, score in zip(spots, scores):
                newest = jnp.maximum(top, jnp.max(score, axis=1, keepdims=True))
                shrink = jnp.exp2(top - newest)
                weight = jnp.exp2(score - newest)
                total = total * shrink + jnp.sum(weight, axis=1, keepdims=True)
                acc[...] = acc[...] * shrink + nn_dot(weight.astype(jnp.bfloat16), kbuf[spot, :LAT])
                top = newest
            return top, total

        top, total = lax.fori_loop(0, KEYS // (2 * CHUNK), body, (top, total))
        context = (acc[...] / total).astype(jnp.bfloat16)
        for k in range(2):
            cols = pl.ds((2 * g + k) * VDIM, VDIM)
            done = nn_dot(context[k * TOK : (k + 1) * TOK], wuv[:, cols])
            hog[g, x, :, k * VDIM : (k + 1) * VDIM] = done.astype(jnp.bfloat16)
        for d in (2, 1, 3):
            send(hog.at[g, x], hog.at[g, x], pair_of(a_sem, g, d), at(dx=d))
        if g == 0:
            serve_w(1)
            serve_w(2)
        if g == PAIRS - 1:
            serve_w(3)
            serve_w(4)

    for g in range(PAIRS):
        for d in (1, 2, 3):
            arrived(hog.at[g, lax.rem(x + NX - d, NX)], pair_of(a_sem, g, d), at(dx=-d))

    def project(zz):
        total = None
        for g in range(PAIRS):
            term = nn_dot(hog[g].reshape(NX * TOK, 2 * VDIM), wbuf[zz, pl.ds(g * 2 * VDIM, 2 * VDIM), :])
            total = term if total is None else total + term
        return total

    tilt = 1 - 2 * lax.rem(z, 2)
    ahead = []
    for n in range(NY):
        if n == 2:
            serve_w(5)
            serve_w(6)
        if n == 3:
            serve_w(7)
        step = (0, -tilt, tilt, 2)[n]
        j = lax.rem(z // 2 + NY + step, NY)
        c1s[n] = project(2 * j + other).astype(jnp.bfloat16)
        send(c1s.at[n], c1r.at[n], pair_of(c1_sem, n), partner)
        kept = project(2 * j + core)
        arrived(c1r.at[n], pair_of(c1_sem, n), partner)
        c2s[n] = (kept + c1r[n].astype(jnp.float32)).astype(jnp.bfloat16)
        onward = copy(c2s.at[n], c2r.at[y], (c2_sem.at[0, n], c2_sem.at[1, y]), (z, x, j, core))
        ahead.append((j, onward))

        @pl.when(j != y)
        def _():
            onward.start()

        @pl.when(j == y)
        def _():
            c2r[y] = c2s[n]

    for d in (1, 2, 3):
        yy = lax.rem(y + d, NY)
        arrived(c2r.at[yy], (c2_sem.at[0, 0], c2_sem.at[1, yy]), at(dy=d))
    summed = c2r[0].astype(jnp.float32)
    for k in range(1, NY):
        summed = summed + c2r[k].astype(jnp.float32)
    c3s[...] = summed.astype(jnp.bfloat16).reshape(NX, TOK, COLS)
    for d in (2, 1, 3):
        send(c3s.at[lax.rem(x + d, NX)], c3r.at[x], pair_of(c3_sem, d), at(dx=d))
    c3r[x] = c3s[x]
    for d in (1, 2, 3):
        arrived(c3r.at[lax.rem(x + NX - d, NX)], pair_of(c3_sem, d), at(dx=-d))
    out[...] = jnp.concatenate([c3r[k].astype(jnp.float32) for k in range(NX)], axis=1).astype(jnp.bfloat16)

    @pl.when(core * y != 0)
    def _():
        shift.wait_send()

    for j, onward in ahead:

        @pl.when(j != y)
        def _():
            onward.wait_send()

    for made in sent:
        made.wait_send()


def local(q_nope, q_rope, latent, k_rope, span_order, w_uk, w_uv, w_o):
    bf16, f32 = jnp.bfloat16, jnp.float32
    dma = pltpu.SemaphoreType.DMA
    vmem = pl.BlockSpec(memory_space=pltpu.VMEM)
    return pl.pallas_call(
        kernel,
        out_shape=jax.ShapeDtypeStruct((TOK, NX * COLS), bf16),
        in_specs=[vmem] * 8,
        out_specs=vmem,
        scratch_shapes=[
            pltpu.VMEM((KEYS, WIDE), bf16),
            pltpu.VMEM((SPAN, WIDE), bf16),
            pltpu.VMEM((TOK, 2 * ROPE), bf16),
            pltpu.VMEM((PAIRS, 2 * TOK, WIDE), bf16),
            pltpu.VMEM((2 * TOK, LAT), f32),
            pltpu.VMEM((NZ, HEADS * VDIM, COLS), bf16),
            pltpu.VMEM((PAIRS, NX, TOK, 2 * VDIM), bf16),
            pltpu.VMEM((NY, NX * TOK, COLS), bf16),
            pltpu.VMEM((NY, NX * TOK, COLS), bf16),
            pltpu.VMEM((NY, NX * TOK, COLS), bf16),
            pltpu.VMEM((NY, NX * TOK, COLS), bf16),
            pltpu.VMEM((NX, TOK, COLS), bf16),
            pltpu.VMEM((NX, TOK, COLS), bf16),
            dma((2,)),
            dma((2, NZ)),
            dma((2, 3, NZ)),
            dma((2, 4, NZ)),
            dma((2, 2, NZ)),
            dma((2, PAIRS, NX)),
            dma((2, NY)),
            dma((2, NY)),
            dma((2, NX)),
        ],
        compiler_params=pltpu.CompilerParams(
            collective_id=0, has_side_effects=True, vmem_limit_bytes=48 * 1024 * 1024
        ),
        cost_estimate=pl.CostEstimate(flops=11_000_000_000, bytes_accessed=4_000_000, transcendentals=4_200_000),
    )(q_nope, q_rope, latent, k_rope, span_order.reshape(1, -1), w_uk, w_uv, w_o)


def solution(mesh):
    torus = Mesh(mesh.devices.reshape(NZ, NX, NY, 2), ("z", "x", "y", "core"))
    ctx, head = ("z", "x"), ("y", "core")
    in_specs = (
        P(ctx, head),
        P(ctx, head),
        P(ctx, None),
        P(ctx, None),
        P(),
        P(None, head),
        P(None, head),
        P(head, ctx),
    )
    return jax.shard_map(local, mesh=torus, in_specs=in_specs, out_specs=P(ctx, head), check_vma=False)
```

```python
import math

import jax
import jax.numpy as jnp
from jax import lax
from jax.experimental import pallas as pl
from jax.experimental.pallas import tpu as pltpu
from jax.sharding import Mesh
from jax.sharding import PartitionSpec as P

NZ, NX, NY = 8, 4, 4
TOK, SPAN, SPANS = 128, 64, 64
HEADS, NOPE, ROPE, LAT, VDIM = 8, 128, 64, 512, 128
WIDE = LAT + ROPE + SPANS
QUERIES = HEADS * TOK
COLS = 224
KEYS = NZ * NX * TOK
STRIP = TOK // (2 * NY)
BUNDLE = NZ * STRIP
CHUNK = 4 * BUNDLE
FACTOR = math.log2(math.e) / math.sqrt(NOPE + ROPE)
HIDDEN = -1e30
MESH = pl.DeviceIdType.MESH
DELTAS = (0, -1, 1, -2, 2, -3, 3, -4)


def nt_dot(a, b):
    return lax.dot_general(a, b, (((1,), (1,)), ((), ())), preferred_element_type=jnp.float32)


def tn_dot(a, b):
    return lax.dot_general(a, b, (((0,), (0,)), ((), ())), preferred_element_type=jnp.float32)


def nn_dot(a, b):
    return jnp.dot(a, b, preferred_element_type=jnp.float32)


def kernel(
    lat, kr, order, qn_in, qr_in, wuk_in, wuv_in, wo_in, out,
    qn, qr, wuk, wuv, kbuf, own_rope, qaug, acc, wuv_t, wbuf, hog, hog_t, c1s, c1r, c2s, c2r, c3s, c3r,
    in_sem, z_sem, w1_sem, w2_sem, p_sem, o_sem, a_sem, c1_sem, c2_sem, c3_sem,
):
    z, x, y, core = (lax.axis_index(n) for n in ("z", "x", "y", "core"))
    other = 1 - core

    def at(dz=0, dx=0, dy=0):
        return (lax.rem(z + NZ + dz, NZ), lax.rem(x + NX + dx, NX), lax.rem(y + NY + dy, NY), core)

    partner = (z, x, y, other)
    peers = [partner] + [at(dz=d) for d in range(1, NZ)]
    peers += [at(dx=d) for d in (1, 2, 3)] + [at(dy=d) for d in (1, 2, 3)]
    barrier = pltpu.get_barrier_semaphore()
    for peer in peers:
        pl.semaphore_signal(barrier, inc=1, device_id=peer, device_id_type=MESH)

    loads = []
    for n, (src, dst) in enumerate(
        ((wo_in, wbuf.at[z]), (wuk_in, wuk), (qn_in, qn), (qr_in, qr), (wuv_in, wuv))
    ):
        loads.append(pltpu.make_async_copy(src, dst, in_sem.at[n]))
        loads[-1].start()

    sent = []

    def copy(src, dst, sems, device):
        return pltpu.make_async_remote_copy(
            src_ref=src, dst_ref=dst, send_sem=sems[0], recv_sem=sems[1], device_id=device, device_id_type=MESH
        )

    def send(src, dst, sems, device):
        made = copy(src, dst, sems, device)
        made.start()
        sent.append(made)

    def arrived(dst, sems, device):
        copy(dst, dst, sems, device).wait_recv()

    def pair_of(sems, *index):
        return sems.at[(0, *index)], sems.at[(1, *index)]

    def base(k, a, b):
        first = x * (1 - k) + y * k + a + 4
        second = y * (1 - k) + x * k + b + 4
        return ((k * 4 + lax.rem(second, 4)) * 4 + lax.rem(first, 4)) * BUNDLE

    def bundle(k, a, b):
        return kbuf.at[pl.ds(pl.multiple_of(base(k, a, b), BUNDLE), BUNDLE)]

    def chunk(k, b):
        second = y * (1 - k) + x * k + b + 4
        return pl.ds(pl.multiple_of((k * 4 + lax.rem(second, 4)) * CHUNK, CHUNK), CHUNK)

    def along1(step):
        return at(dx=other * step, dy=core * step)

    def along2(step):
        return at(dx=core * step, dy=other * step)

    def strip(dz):
        start = base(core, 0, 0) + lax.rem(z + NZ + dz, NZ) * STRIP
        return pl.ds(pl.multiple_of(start, STRIP), STRIP)

    own_rope[...] = jnp.zeros_like(own_rope)
    own_rope[:, :ROPE] = kr[...].astype(jnp.float32).T.astype(jnp.bfloat16)
    mine = pl.ds(pl.multiple_of((2 * y + core) * STRIP, STRIP), STRIP)
    own_slot = (z * NX + x) * 2 + y // 2
    lane = lax.broadcasted_iota(jnp.int32, (STRIP, ROPE + SPANS), 1)
    kbuf[strip(0), :LAT] = lat[mine, :]
    kbuf[strip(0), LAT:] = jnp.where(
        lane == ROPE + own_slot, 1.0, own_rope[mine, :].astype(jnp.float32)
    ).astype(jnp.bfloat16)

    pl.semaphore_wait(barrier, len(peers))

    for d in (4, 3, 5, 2, 6, 1, 7):
        send(kbuf.at[strip(0)], kbuf.at[strip(0)], pair_of(z_sem, d), at(dz=d))

    tone = 1 - 2 * core
    ahead_z, behind_z = at(dz=tone), at(dz=-tone)

    def wpart(delta, half):
        zz = lax.rem(z + NZ + tone * delta, NZ)
        return wbuf.at[zz, pl.ds(half * (COLS // 2), COLS // 2)]

    def send_w(i, later, half):
        here = wpart(DELTAS[i], half)
        send(here, here, pair_of(o_sem, half, later), ahead_z if DELTAS[later] < 0 else behind_z)

    def wait_w(i, half):
        arrived(wpart(DELTAS[i], half), pair_of(o_sem, half, i), ahead_z if DELTAS[i] > 0 else behind_z)

    def serve_w(i, half):
        wait_w(i, half)
        if i + 2 < NZ:
            send_w(i, i + 2, half)

    loads[0].wait()
    for half in range(2):
        send_w(0, 1, half)
        send_w(0, 2, half)

    square = (SPANS, SPANS)
    places = order[...]
    diagonal = lax.broadcasted_iota(jnp.int32, square, 0) == lax.broadcasted_iota(jnp.int32, square, 1)
    column = jnp.sum(jnp.where(diagonal, jnp.broadcast_to(places, square), 0), axis=1, keepdims=True)
    slot_row = lax.broadcasted_iota(jnp.int32, (SPANS, TOK), 0)
    own_half = lax.broadcasted_iota(jnp.int32, (SPANS, TOK), 1) // SPAN
    own = slot_row == (z * NX + x) * 2 + own_half
    column = jnp.broadcast_to(column, (SPANS, TOK))
    place = jnp.sum(jnp.where(own, column, 0), axis=0, keepdims=True)
    mask = jnp.where(column >= place, HIDDEN, 0.0).astype(jnp.bfloat16)
    for n in (1, 2, 3):
        loads[n].wait()
    rot = qr[...].astype(jnp.float32).T.astype(jnp.bfloat16)
    for h in range(HEADS):
        cols = slice(h * TOK, (h + 1) * TOK)
        qaug[:LAT, cols] = nt_dot(wuk[:, cols], qn[:, cols]).astype(jnp.bfloat16)
        qaug[LAT : LAT + ROPE, cols] = rot[h * ROPE : (h + 1) * ROPE]
        qaug[LAT + ROPE :, cols] = mask

    def hand_on(a, first):
        here = bundle(core, a, 0)
        if first:
            for s in (2, 1, 3):
                send(here, here, pair_of(w1_sem, s), along1(s))
        for s in (2, 1, 3):
            send(here, here, pair_of(w2_sem, s, a), along2(s))
        send(here, here, pair_of(p_sem, 0, a), partner)

    def come(b):
        s = (4 - b) % 4
        for a in range(4):
            here = bundle(core, a, b)
            arrived(here, pair_of(w2_sem, s, a), along2(b))
            send(here, here, pair_of(p_sem, b, a), partner)

    def partner_has(b):
        for a in range(4):
            arrived(bundle(other, a, b), pair_of(p_sem, b, a), partner)

    def attend(spots, lo, size, top, total):
        cols = slice(lo, lo + size)
        scores = [nn_dot(kbuf[spot, :], qaug[:, cols]) * FACTOR for spot in spots]
        for spot, score in zip(spots, scores):
            newest = jnp.maximum(top, jnp.max(score, axis=0, keepdims=True))
            shrink = jnp.exp2(top - newest)
            weight = jnp.exp2(score - newest)
            total = total * shrink + jnp.sum(weight.reshape(CHUNK // 8, 8, size), axis=0)
            acc[:, cols] = acc[:, cols] * shrink + tn_dot(kbuf[spot, :LAT], weight.astype(jnp.bfloat16))
            top = newest
        return top, total

    for d in range(1, NZ):
        arrived(kbuf.at[strip(-d)], pair_of(z_sem, d), at(dz=-d))
    hand_on(0, True)

    row = lax.broadcasted_iota(jnp.int32, (TOK, QUERIES), 0)
    col = lax.rem(lax.broadcasted_iota(jnp.int32, (TOK, QUERIES), 1), TOK)
    seen = (row <= col) & (row >= (col // SPAN) * SPAN)
    score = nn_dot(lat[...], qaug[:LAT, :]) + nn_dot(own_rope[...], qaug[LAT:, :])
    score = jnp.where(seen, score * FACTOR, HIDDEN)
    top = jnp.max(score, axis=0, keepdims=True)
    weight = jnp.exp2(score - top)
    total = jnp.sum(weight.reshape(TOK // 8, 8, QUERIES), axis=0)
    acc[...] = tn_dot(lat[...], weight.astype(jnp.bfloat16))
    loads[4].wait()
    wuv_t[...] = wuv[...].T

    WING = QUERIES // 2
    state = [(top[:, n * WING : (n + 1) * WING], total[:, n * WING : (n + 1) * WING]) for n in range(2)]

    def attend_all(spot):
        for n in range(2):
            state[n] = attend([spot], n * WING, WING, *state[n])

    for a in (1, 3, 2):
        arrived(bundle(core, a, 0), pair_of(w1_sem, (4 - a) % 4), along1(a))
        hand_on(a, False)
    serve_w(1, 0)
    serve_w(2, 0)
    attend_all(chunk(core, 0))
    partner_has(0)
    attend_all(chunk(other, 0))
    serve_w(1, 1)
    serve_w(2, 1)
    come(1)
    attend_all(chunk(core, 1))
    come(3)
    attend_all(chunk(core, 3))
    serve_w(3, 0)
    serve_w(4, 0)
    partner_has(1)
    attend_all(chunk(other, 1))
    come(2)
    partner_has(3)
    attend_all(chunk(other, 3))
    attend_all(chunk(core, 2))
    serve_w(3, 1)
    serve_w(4, 1)
    partner_has(2)

    def send_heads(half, n):
        here = hog.at[half, x, :, n * WING : (n + 1) * WING]
        for d in (2, 1, 3):
            send(here, here, pair_of(a_sem, half, n, d), at(dx=d))

    for n in range(2):
        top, total = attend([chunk(other, 2)], n * WING, WING, *state[n])
        whole = jnp.sum(total, axis=0, keepdims=True)
        context = (acc[:, n * WING : (n + 1) * WING] / whole).astype(jnp.bfloat16)
        for k in range(HEADS // 2):
            spot = slice((n * HEADS // 2 + k) * VDIM, (n * HEADS // 2 + k + 1) * VDIM)
            done = nn_dot(wuv_t[spot, :], context[:, k * TOK : (k + 1) * TOK]).T.astype(jnp.bfloat16)
            for half in range(2):
                hog[half, x, :, spot] = done[half * SPAN : (half + 1) * SPAN]
        send_heads(0, n)
    for n in range(2):
        send_heads(1, n)
    for half in range(2):
        serve_w(5, half)
        serve_w(6, half)

    tilt = 1 - 2 * lax.rem(z, 2)
    order_y = [lax.rem(z // 2 + NY + step, NY) for step in (0, -tilt, tilt, 2)]
    ahead = []
    for half in range(2):
        for n in range(2):
            for d in (1, 2, 3):
                here = hog.at[half, lax.rem(x + NX - d, NX), :, n * WING : (n + 1) * WING]
                arrived(here, pair_of(a_sem, half, n, d), at(dx=-d))
        hog_t[...] = hog[half].reshape(NX * SPAN, HEADS * VDIM).T
        if half == 0:
            wait_w(7, 0)
            wait_w(7, 1)
        for n, j in enumerate(order_y):
            c1s[half, n] = nn_dot(wbuf[2 * j + other], hog_t[...]).astype(jnp.bfloat16)
            send(c1s.at[half, n], c1r.at[half, n], pair_of(c1_sem, half, n), partner)
        for n, j in enumerate(order_y):
            kept = nn_dot(wbuf[2 * j + core], hog_t[...])
            arrived(c1r.at[half, n], pair_of(c1_sem, half, n), partner)
            c2s[half, n] = (kept + c1r[half, n].astype(jnp.float32)).astype(jnp.bfloat16)
            sems = (c2_sem.at[0, half, n], c2_sem.at[1, half, y])
            onward = copy(c2s.at[half, n], c2r.at[half, y], sems, (z, x, j, core))
            ahead.append((j, onward))

            @pl.when(j != y)
            def _():
                onward.start()

            @pl.when(j == y)
            def _():
                c2r[half, y] = c2s[half, n]

    sums = []
    for half in range(2):
        for d in (1, 2, 3):
            yy = lax.rem(y + d, NY)
            arrived(c2r.at[half, yy], (c2_sem.at[0, half, 0], c2_sem.at[1, half, yy]), at(dy=d))
        summed = c2r[half, 0].astype(jnp.float32)
        for k in range(1, NY):
            summed = summed + c2r[half, k].astype(jnp.float32)
        sums.append(summed)
    for k in range(NX):
        both = [summed[:, k * SPAN : (k + 1) * SPAN] for summed in sums]
        c3s[k] = jnp.concatenate(both, axis=1).astype(jnp.bfloat16)
    for d in (2, 1, 3):
        send(c3s.at[lax.rem(x + d, NX)], c3r.at[x], pair_of(c3_sem, d), at(dx=d))
    c3r[x] = c3s[x]
    for d in (1, 2, 3):
        arrived(c3r.at[lax.rem(x + NX - d, NX)], pair_of(c3_sem, d), at(dx=-d))
    out[...] = c3r[...].reshape(NX * COLS, TOK).astype(jnp.float32).T.astype(jnp.bfloat16)

    for j, onward in ahead:

        @pl.when(j != y)
        def _():
            onward.wait_send()

    for made in sent:
        made.wait_send()


def local(q_nope, q_rope, latent, k_rope, span_order, w_uk, w_uv, w_o):
    bf16, f32 = jnp.bfloat16, jnp.float32
    dma = pltpu.SemaphoreType.DMA
    vmem = pl.BlockSpec(memory_space=pltpu.VMEM)
    anywhere = pl.BlockSpec(memory_space=pl.ANY)
    return pl.pallas_call(
        kernel,
        out_shape=jax.ShapeDtypeStruct((TOK, NX * COLS), bf16),
        in_specs=[vmem] * 3 + [anywhere] * 5,
        out_specs=vmem,
        scratch_shapes=[
            pltpu.VMEM((TOK, HEADS * NOPE), bf16),
            pltpu.VMEM((TOK, HEADS * ROPE), bf16),
            pltpu.VMEM((LAT, HEADS * NOPE), bf16),
            pltpu.VMEM((LAT, HEADS * VDIM), bf16),
            pltpu.VMEM((KEYS, WIDE), bf16),
            pltpu.VMEM((TOK, ROPE + SPANS), bf16),
            pltpu.VMEM((WIDE, QUERIES), bf16),
            pltpu.VMEM((LAT, QUERIES), f32),
            pltpu.VMEM((HEADS * VDIM, LAT), bf16),
            pltpu.VMEM((NZ, COLS, HEADS * VDIM), bf16),
            pltpu.VMEM((2, NX, SPAN, HEADS * VDIM), bf16),
            pltpu.VMEM((HEADS * VDIM, NX * SPAN), bf16),
            pltpu.VMEM((2, NY, COLS, NX * SPAN), bf16),
            pltpu.VMEM((2, NY, COLS, NX * SPAN), bf16),
            pltpu.VMEM((2, NY, COLS, NX * SPAN), bf16),
            pltpu.VMEM((2, NY, COLS, NX * SPAN), bf16),
            pltpu.VMEM((NX, COLS, TOK), bf16),
            pltpu.VMEM((NX, COLS, TOK), bf16),
            dma((5,)),
            dma((2, NZ)),
            dma((2, 4)),
            dma((2, 4, 4)),
            dma((2, 4, 4)),
            dma((2, 2, NZ)),
            dma((2, 2, 2, NX)),
            dma((2, 2, NY)),
            dma((2, 2, NY)),
            dma((2, NX)),
        ],
        compiler_params=pltpu.CompilerParams(
            collective_id=0, has_side_effects=True, vmem_limit_bytes=56 * 1024 * 1024
        ),
        cost_estimate=pl.CostEstimate(flops=11_000_000_000, bytes_accessed=4_000_000, transcendentals=4_200_000),
    )(latent, k_rope.T, span_order.reshape(1, -1), q_nope, q_rope, w_uk, w_uv, w_o.T)


def solution(mesh):
    torus = Mesh(mesh.devices.reshape(NZ, NX, NY, 2), ("z", "x", "y", "core"))
    ctx, head = ("z", "x"), ("y", "core")
    in_specs = (
        P(ctx, head),
        P(ctx, head),
        P(ctx, None),
        P(ctx, None),
        P(),
        P(None, head),
        P(None, head),
        P(head, ctx),
    )
    return jax.shard_map(local, mesh=torus, in_specs=in_specs, out_specs=P(ctx, head), check_vma=False)
```

```python
import math

import jax
import jax.numpy as jnp
from jax import lax
from jax.experimental import pallas as pl
from jax.experimental.pallas import tpu as pltpu
from jax.sharding import Mesh
from jax.sharding import PartitionSpec as P

NZ, NX, NY = 8, 4, 4
TOK, SPAN, SPANS = 128, 64, 64
HEADS, NOPE, ROPE, LAT, VDIM = 8, 128, 64, 512, 128
WIDE = LAT + ROPE + SPANS
QUERIES = HEADS * TOK
COLS = 224
KEYS = NZ * NX * TOK
STRIP = TOK // (2 * NY)
BUNDLE = NZ * STRIP
GROUP = BUNDLE // 2
PLACES = {0: 0, 1: 1, 7: 2, 2: 3, 6: 4, 3: 5, 5: 6, 4: 7}
CHUNK = 4 * BUNDLE
FACTOR = math.log2(math.e) / math.sqrt(NOPE + ROPE)
HIDDEN = -1e30
MESH = pl.DeviceIdType.MESH
DELTAS = (0, -1, 1, -2, 2, -3, 3, -4)


def nt_dot(a, b):
    return lax.dot_general(a, b, (((1,), (1,)), ((), ())), preferred_element_type=jnp.float32)


def tn_dot(a, b):
    return lax.dot_general(a, b, (((0,), (0,)), ((), ())), preferred_element_type=jnp.float32)


def nn_dot(a, b):
    return jnp.dot(a, b, preferred_element_type=jnp.float32)


def kernel(
    lat, kr, order, qn_in, qr_in, wuk_in, wuv_in, wo_in, out,
    qn, qr, wuk, wuv, kbuf, own_rope, qaug, acc, wuv_t, wbuf, hog, c1s, c1r, c2s, c2r, c3s, c3r,
    in_sem, z_sem, w1_sem, w2_sem, p_sem, o_sem, a_sem, c1_sem, c2_sem, c3_sem,
):
    z, x, y, core = (lax.axis_index(n) for n in ("z", "x", "y", "core"))
    other = 1 - core

    def at(dz=0, dx=0, dy=0):
        return (lax.rem(z + NZ + dz, NZ), lax.rem(x + NX + dx, NX), lax.rem(y + NY + dy, NY), core)

    partner = (z, x, y, other)
    peers = [partner] + [at(dz=d) for d in range(1, NZ)]
    peers += [at(dx=d) for d in (1, 2, 3)] + [at(dy=d) for d in (1, 2, 3)]
    barrier = pltpu.get_barrier_semaphore()
    for peer in peers:
        pl.semaphore_signal(barrier, inc=1, device_id=peer, device_id_type=MESH)

    loads = []
    for n, (src, dst) in enumerate(
        ((wo_in, wbuf.at[z]), (wuk_in, wuk), (qn_in, qn), (qr_in, qr), (wuv_in, wuv))
    ):
        loads.append(pltpu.make_async_copy(src, dst, in_sem.at[n]))
        loads[-1].start()

    sent = []

    def copy(src, dst, sems, device):
        return pltpu.make_async_remote_copy(
            src_ref=src, dst_ref=dst, send_sem=sems[0], recv_sem=sems[1], device_id=device, device_id_type=MESH
        )

    def send(src, dst, sems, device):
        made = copy(src, dst, sems, device)
        made.start()
        sent.append(made)

    def arrived(dst, sems, device):
        copy(dst, dst, sems, device).wait_recv()

    def pair_of(sems, *index):
        return sems.at[(0, *index)], sems.at[(1, *index)]

    def base(k, a, b):
        first = x * (1 - k) + y * k + a + 4
        second = y * (1 - k) + x * k + b + 4
        return ((k * 4 + lax.rem(second, 4)) * 4 + lax.rem(first, 4)) * BUNDLE

    def bundle(k, a, b):
        return kbuf.at[pl.ds(pl.multiple_of(base(k, a, b), BUNDLE), BUNDLE)]

    def group(a, b, n):
        return kbuf.at[pl.ds(pl.multiple_of(base(core, a, b) + n * GROUP, GROUP), GROUP)]

    def chunk(k, b):
        second = y * (1 - k) + x * k + b + 4
        return pl.ds(pl.multiple_of((k * 4 + lax.rem(second, 4)) * CHUNK, CHUNK), CHUNK)

    def along1(step):
        return at(dx=other * step, dy=core * step)

    def along2(step):
        return at(dx=core * step, dy=other * step)

    def strip(dz):
        start = base(core, 0, 0) + PLACES[dz % NZ] * STRIP
        return pl.ds(pl.multiple_of(start, STRIP), STRIP)

    own_rope[...] = jnp.zeros_like(own_rope)
    own_rope[:, :ROPE] = kr[...].astype(jnp.float32).T.astype(jnp.bfloat16)
    mine = pl.ds(pl.multiple_of((2 * y + core) * STRIP, STRIP), STRIP)
    own_slot = (z * NX + x) * 2 + y // 2
    lane = lax.broadcasted_iota(jnp.int32, (STRIP, ROPE + SPANS), 1)
    kbuf[strip(0), :LAT] = lat[mine, :]
    kbuf[strip(0), LAT:] = jnp.where(
        lane == ROPE + own_slot, 1.0, own_rope[mine, :].astype(jnp.float32)
    ).astype(jnp.bfloat16)

    pl.semaphore_wait(barrier, len(peers))

    for d in (6, 7, 1, 2, 4, 5, 3):
        send(kbuf.at[strip(0)], kbuf.at[strip(-d)], pair_of(z_sem, d), at(dz=d))

    tone = 1 - 2 * core
    ahead_z, behind_z = at(dz=tone), at(dz=-tone)

    def wpart(delta, half):
        zz = lax.rem(z + NZ + tone * delta, NZ)
        return wbuf.at[zz, pl.ds(half * (COLS // 2), COLS // 2)]

    def send_w(i, later, half):
        here = wpart(DELTAS[i], half)
        send(here, here, pair_of(o_sem, half, later), ahead_z if DELTAS[later] < 0 else behind_z)

    def wait_w(i, half):
        arrived(wpart(DELTAS[i], half), pair_of(o_sem, half, i), ahead_z if DELTAS[i] > 0 else behind_z)

    def serve_w(i, half):
        wait_w(i, half)
        if i + 2 < NZ:
            send_w(i, i + 2, half)

    loads[0].wait()
    for half in range(2):
        send_w(0, 1, half)
        send_w(0, 2, half)

    square = (SPANS, SPANS)
    places = order[...]
    diagonal = lax.broadcasted_iota(jnp.int32, square, 0) == lax.broadcasted_iota(jnp.int32, square, 1)
    column = jnp.sum(jnp.where(diagonal, jnp.broadcast_to(places, square), 0), axis=1, keepdims=True)
    slot_row = lax.broadcasted_iota(jnp.int32, (SPANS, TOK), 0)
    own_half = lax.broadcasted_iota(jnp.int32, (SPANS, TOK), 1) // SPAN
    own = slot_row == (z * NX + x) * 2 + own_half
    column = jnp.broadcast_to(column, (SPANS, TOK))
    place = jnp.sum(jnp.where(own, column, 0), axis=0, keepdims=True)
    mask = jnp.where(column >= place, HIDDEN, 0.0).astype(jnp.bfloat16)
    for n in (1, 2, 3):
        loads[n].wait()
    rot = qr[...].astype(jnp.float32).T.astype(jnp.bfloat16)
    for h in range(HEADS):
        cols = slice(h * TOK, (h + 1) * TOK)
        qaug[:LAT, cols] = nt_dot(wuk[:, cols], qn[:, cols]).astype(jnp.bfloat16)
        qaug[LAT : LAT + ROPE, cols] = rot[h * ROPE : (h + 1) * ROPE]
        qaug[LAT + ROPE :, cols] = mask

    def hand_on(a, n):
        here = group(a, 0, n)
        if a == 0:
            for s in (2, 1, 3):
                send(here, here, pair_of(w1_sem, n, s), along1(s))
        for s in (2, 1, 3):
            send(here, here, pair_of(w2_sem, n, s, a), along2(s))
        if n:
            send(bundle(core, a, 0), bundle(core, a, 0), pair_of(p_sem, 0, a), partner)

    def first_round(n):
        for a in (1, 3, 2):
            arrived(group(a, 0, n), pair_of(w1_sem, n, (4 - a) % 4), along1(a))
            hand_on(a, n)

    def from_z(n):
        for d, place in PLACES.items():
            if d and place // 4 == n:
                arrived(kbuf.at[strip(d)], pair_of(z_sem, NZ - d), at(dz=d))
        hand_on(0, n)

    def come(b):
        for a in (0, 1, 3, 2):
            for n in range(2):
                arrived(group(a, b, n), pair_of(w2_sem, n, (4 - b) % 4, a), along2(b))
            send(bundle(core, a, b), bundle(core, a, b), pair_of(p_sem, b, a), partner)

    def partner_has(b):
        for a in range(4):
            arrived(bundle(other, a, b), pair_of(p_sem, b, a), partner)

    def attend(spots, lo, size, top, total):
        cols = slice(lo, lo + size)
        scores = [nn_dot(kbuf[spot, :], qaug[:, cols]) * FACTOR for spot in spots]
        for spot, score in zip(spots, scores):
            newest = jnp.maximum(top, jnp.max(score, axis=0, keepdims=True))
            shrink = jnp.exp2(top - newest)
            weight = jnp.exp2(score - newest)
            total = total * shrink + jnp.sum(weight.reshape(CHUNK // 8, 8, size), axis=0)
            acc[:, cols] = acc[:, cols] * shrink + tn_dot(kbuf[spot, :LAT], weight.astype(jnp.bfloat16))
            top = newest
        return top, total

    from_z(0)
    from_z(1)
    first_round(0)

    row = lax.broadcasted_iota(jnp.int32, (TOK, QUERIES), 0)
    col = lax.rem(lax.broadcasted_iota(jnp.int32, (TOK, QUERIES), 1), TOK)
    seen = (row <= col) & (row >= (col // SPAN) * SPAN)
    score = nn_dot(lat[...], qaug[:LAT, :]) + nn_dot(own_rope[...], qaug[LAT:, :])
    score = jnp.where(seen, score * FACTOR, HIDDEN)
    top = jnp.max(score, axis=0, keepdims=True)
    weight = jnp.exp2(score - top)
    total = jnp.sum(weight.reshape(TOK // 8, 8, QUERIES), axis=0)
    acc[...] = tn_dot(lat[...], weight.astype(jnp.bfloat16))
    loads[4].wait()
    wuv_t[...] = wuv[...].T

    WING = QUERIES // 2
    state = [(top[:, n * WING : (n + 1) * WING], total[:, n * WING : (n + 1) * WING]) for n in range(2)]

    def attend_all(spot):
        for n in range(2):
            state[n] = attend([spot], n * WING, WING, *state[n])

    first_round(1)
    serve_w(1, 0)
    serve_w(2, 0)
    attend_all(chunk(core, 0))
    partner_has(0)
    attend_all(chunk(other, 0))
    serve_w(1, 1)
    serve_w(2, 1)
    come(1)
    attend_all(chunk(core, 1))
    come(3)
    attend_all(chunk(core, 3))
    serve_w(3, 0)
    serve_w(4, 0)
    partner_has(1)
    attend_all(chunk(other, 1))
    come(2)
    partner_has(3)
    attend_all(chunk(other, 3))
    attend_all(chunk(core, 2))
    serve_w(3, 1)
    serve_w(4, 1)
    partner_has(2)

    for n in range(2):
        half = slice(n * WING, (n + 1) * WING)
        top, total = attend([chunk(other, 2)], n * WING, WING, *state[n])
        whole = jnp.sum(total, axis=0, keepdims=True)
        context = (acc[:, half] / whole).astype(jnp.bfloat16)
        for k in range(HEADS // 2):
            spot = slice((n * HEADS // 2 + k) * VDIM, (n * HEADS // 2 + k + 1) * VDIM)
            hog[x, spot] = nn_dot(wuv_t[spot, :], context[:, k * TOK : (k + 1) * TOK]).astype(jnp.bfloat16)
        for d in (1, 3, 2):
            send(hog.at[x, half], hog.at[x, half], pair_of(a_sem, n, d), at(dx=d))
    for half in range(2):
        serve_w(5, half)
        serve_w(6, half)
    for half in range(2):
        wait_w(7, half)

    tilt = 1 - 2 * lax.rem(z, 2)
    order_y = [lax.rem(z // 2 + NY + step, NY) for step in (0, -tilt, tilt, 2)]
    ahead = []

    def project(o):
        block = lax.rem(x + o, NX)
        if o:
            for n in range(2):
                arrived(hog.at[block, n * WING : (n + 1) * WING], pair_of(a_sem, n, NX - o), at(dx=o))
        for n, j in enumerate(order_y):
            c1s[o, n] = nn_dot(wbuf[2 * j + other], hog[block]).astype(jnp.bfloat16)
            send(c1s.at[o, n], c1r.at[o, n], pair_of(c1_sem, o, n), partner)
        for n, j in enumerate(order_y):
            kept = nn_dot(wbuf[2 * j + core], hog[block])
            arrived(c1r.at[o, n], pair_of(c1_sem, o, n), partner)
            c2s[o, n] = (kept + c1r[o, n].astype(jnp.float32)).astype(jnp.bfloat16)
            sems = (c2_sem.at[0, o, n], c2_sem.at[1, o, y])
            onward = copy(c2s.at[o, n], c2r.at[o, y], sems, (z, x, j, core))
            ahead.append((j, onward))

            @pl.when(j != y)
            def _():
                onward.start()

            @pl.when(j == y)
            def _():
                c2r[o, y] = c2s[o, n]

    def collect(o):
        for d in (1, 2, 3):
            yy = lax.rem(y + d, NY)
            arrived(c2r.at[o, yy], (c2_sem.at[0, o, 0], c2_sem.at[1, o, yy]), at(dy=d))
        summed = c2r[o, 0].astype(jnp.float32)
        for k in range(1, NY):
            summed = summed + c2r[o, k].astype(jnp.float32)
        if o:
            c3s[o] = summed.astype(jnp.bfloat16)
            send(c3s.at[o], c3r.at[x], pair_of(c3_sem, o), at(dx=o))
        else:
            c3r[x] = summed.astype(jnp.bfloat16)

    project(0)
    project(1)
    collect(0)
    project(3)
    collect(1)
    project(2)
    collect(3)
    collect(2)
    for d in (1, 2, 3):
        arrived(c3r.at[lax.rem(x + NX - d, NX)], pair_of(c3_sem, d), at(dx=-d))
    out[...] = c3r[...].reshape(NX * COLS, TOK).astype(jnp.float32).T.astype(jnp.bfloat16)

    for j, onward in ahead:

        @pl.when(j != y)
        def _():
            onward.wait_send()

    for made in sent:
        made.wait_send()


def local(q_nope, q_rope, latent, k_rope, span_order, w_uk, w_uv, w_o):
    bf16, f32 = jnp.bfloat16, jnp.float32
    dma = pltpu.SemaphoreType.DMA
    vmem = pl.BlockSpec(memory_space=pltpu.VMEM)
    anywhere = pl.BlockSpec(memory_space=pl.ANY)
    return pl.pallas_call(
        kernel,
        out_shape=jax.ShapeDtypeStruct((TOK, NX * COLS), bf16),
        in_specs=[vmem] * 3 + [anywhere] * 5,
        out_specs=vmem,
        scratch_shapes=[
            pltpu.VMEM((TOK, HEADS * NOPE), bf16),
            pltpu.VMEM((TOK, HEADS * ROPE), bf16),
            pltpu.VMEM((LAT, HEADS * NOPE), bf16),
            pltpu.VMEM((LAT, HEADS * VDIM), bf16),
            pltpu.VMEM((KEYS, WIDE), bf16),
            pltpu.VMEM((TOK, ROPE + SPANS), bf16),
            pltpu.VMEM((WIDE, QUERIES), bf16),
            pltpu.VMEM((LAT, QUERIES), f32),
            pltpu.VMEM((HEADS * VDIM, LAT), bf16),
            pltpu.VMEM((NZ, COLS, HEADS * VDIM), bf16),
            pltpu.VMEM((NX, HEADS * VDIM, TOK), bf16),
            pltpu.VMEM((NX, NY, COLS, TOK), bf16),
            pltpu.VMEM((NX, NY, COLS, TOK), bf16),
            pltpu.VMEM((NX, NY, COLS, TOK), bf16),
            pltpu.VMEM((NX, NY, COLS, TOK), bf16),
            pltpu.VMEM((NX, COLS, TOK), bf16),
            pltpu.VMEM((NX, COLS, TOK), bf16),
            dma((5,)),
            dma((2, NZ)),
            dma((2, 2, 4)),
            dma((2, 2, 4, 4)),
            dma((2, 4, 4)),
            dma((2, 2, NZ)),
            dma((2, 2, NX)),
            dma((2, NX, NY)),
            dma((2, NX, NY)),
            dma((2, NX)),
        ],
        compiler_params=pltpu.CompilerParams(
            collective_id=0, has_side_effects=True, vmem_limit_bytes=56 * 1024 * 1024
        ),
        cost_estimate=pl.CostEstimate(flops=11_000_000_000, bytes_accessed=4_000_000, transcendentals=4_200_000),
    )(latent, k_rope.T, span_order.reshape(1, -1), q_nope, q_rope, w_uk, w_uv, w_o.T)


def solution(mesh):
    torus = Mesh(mesh.devices.reshape(NZ, NX, NY, 2), ("z", "x", "y", "core"))
    ctx, head = ("z", "x"), ("y", "core")
    in_specs = (
        P(ctx, head),
        P(ctx, head),
        P(ctx, None),
        P(ctx, None),
        P(),
        P(None, head),
        P(None, head),
        P(head, ctx),
    )
    return jax.shard_map(local, mesh=torus, in_specs=in_specs, out_specs=P(ctx, head), check_vma=False)
```

```python
import math

import jax
import jax.numpy as jnp
from jax import lax
from jax.experimental import pallas as pl
from jax.experimental.pallas import tpu as pltpu
from jax.sharding import Mesh
from jax.sharding import PartitionSpec as P

NZ, NX, NY = 8, 4, 4
TOK, SPAN, SPANS = 128, 64, 64
HEADS, NOPE, ROPE, LAT, VDIM = 8, 128, 64, 512, 128
WIDE = LAT + ROPE + SPANS
QUERIES = HEADS * TOK
COLS = 224
KEYS = NZ * NX * TOK
STRIP = TOK // (2 * NY)
BUNDLE = NZ * STRIP
GROUP = BUNDLE // 2
PLACES = {0: 0, 1: 1, 7: 2, 2: 3, 6: 4, 3: 5, 5: 6, 4: 7}
CHUNK = 4 * BUNDLE
FACTOR = math.log2(math.e) / math.sqrt(NOPE + ROPE)
HIDDEN = -1e30
MESH = pl.DeviceIdType.MESH
DELTAS = (0, -1, 1, -2, 2, -3, 3, -4)


def nt_dot(a, b):
    return lax.dot_general(a, b, (((1,), (1,)), ((), ())), preferred_element_type=jnp.float32)


def tn_dot(a, b):
    return lax.dot_general(a, b, (((0,), (0,)), ((), ())), preferred_element_type=jnp.float32)


def nn_dot(a, b):
    return jnp.dot(a, b, preferred_element_type=jnp.float32)


def kernel(
    lat, kr, order, qn_in, qr_in, wuk_in, wuv_in, wo_in, out,
    qn, qr, wuk, wuv, kbuf, own_rope, qaug, acc, wuv_t, wbuf, hog, c1s, c1r, c2s, c2r, c3s, c3r,
    in_sem, z_sem, w1_sem, w2_sem, p_sem, o_sem, a_sem, c1_sem, c2_sem, c3_sem,
):
    z, x, y, core = (lax.axis_index(n) for n in ("z", "x", "y", "core"))
    other = 1 - core

    def at(dz=0, dx=0, dy=0):
        return (lax.rem(z + NZ + dz, NZ), lax.rem(x + NX + dx, NX), lax.rem(y + NY + dy, NY), core)

    partner = (z, x, y, other)
    peers = [partner] + [at(dz=d) for d in range(1, NZ)]
    peers += [at(dx=d) for d in (1, 2, 3)] + [at(dy=d) for d in (1, 2, 3)]
    barrier = pltpu.get_barrier_semaphore()
    for peer in peers:
        pl.semaphore_signal(barrier, inc=1, device_id=peer, device_id_type=MESH)

    loads = []
    for n, (src, dst) in enumerate(
        ((wo_in, wbuf.at[z]), (wuk_in, wuk), (qn_in, qn), (qr_in, qr), (wuv_in, wuv))
    ):
        loads.append(pltpu.make_async_copy(src, dst, in_sem.at[n]))
        loads[-1].start()

    sent = []

    def copy(src, dst, sems, device):
        return pltpu.make_async_remote_copy(
            src_ref=src, dst_ref=dst, send_sem=sems[0], recv_sem=sems[1], device_id=device, device_id_type=MESH
        )

    def send(src, dst, sems, device):
        made = copy(src, dst, sems, device)
        made.start()
        sent.append(made)

    def arrived(dst, sems, device):
        copy(dst, dst, sems, device).wait_recv()

    def pair_of(sems, *index):
        return sems.at[(0, *index)], sems.at[(1, *index)]

    def chunk_start(n, b):
        second = (x if n else y) + b + 4
        return (n * 4 + lax.rem(second, 4)) * CHUNK

    def chunk(n, b):
        return pl.ds(pl.multiple_of(chunk_start(n, b), CHUNK), CHUNK)

    def share(k, n, b):
        return kbuf.at[pl.ds(pl.multiple_of(chunk_start(n, b) + k * (CHUNK // 2), CHUNK // 2), CHUNK // 2)]

    def group_start(n, a, b):
        first = (y if n else x) + a + 4
        return chunk_start(n, b) + core * (CHUNK // 2) + lax.rem(first, 4) * GROUP

    def group(n, a, b):
        return kbuf.at[pl.ds(pl.multiple_of(group_start(n, a, b), GROUP), GROUP)]

    def along1(n, step):
        return at(dy=step) if n else at(dx=step)

    def along2(n, step):
        return at(dx=step) if n else at(dy=step)

    def strip(dz):
        place = PLACES[dz % NZ]
        start = group_start(place // 4, 0, 0) + place % 4 * STRIP
        return pl.ds(pl.multiple_of(start, STRIP), STRIP)

    own_rope[...] = jnp.zeros_like(own_rope)
    own_rope[:, :ROPE] = kr[...].astype(jnp.float32).T.astype(jnp.bfloat16)
    mine = pl.ds(pl.multiple_of((2 * y + core) * STRIP, STRIP), STRIP)
    own_slot = (z * NX + x) * 2 + y // 2
    lane = lax.broadcasted_iota(jnp.int32, (STRIP, ROPE + SPANS), 1)
    kbuf[strip(0), :LAT] = lat[mine, :]
    kbuf[strip(0), LAT:] = jnp.where(
        lane == ROPE + own_slot, 1.0, own_rope[mine, :].astype(jnp.float32)
    ).astype(jnp.bfloat16)

    pl.semaphore_wait(barrier, len(peers))

    for d in (6, 7, 1, 2, 4, 5, 3):
        send(kbuf.at[strip(0)], kbuf.at[strip(-d)], pair_of(z_sem, d), at(dz=d))

    tone = 1 - 2 * core
    ahead_z, behind_z = at(dz=tone), at(dz=-tone)

    def wpart(delta, half):
        zz = lax.rem(z + NZ + tone * delta, NZ)
        return wbuf.at[zz, pl.ds(half * (COLS // 2), COLS // 2)]

    def send_w(i, later, half):
        here = wpart(DELTAS[i], half)
        send(here, here, pair_of(o_sem, half, later), ahead_z if DELTAS[later] < 0 else behind_z)

    def wait_w(i, half):
        arrived(wpart(DELTAS[i], half), pair_of(o_sem, half, i), ahead_z if DELTAS[i] > 0 else behind_z)

    def serve_w(i, half):
        wait_w(i, half)
        if i + 2 < NZ:
            send_w(i, i + 2, half)

    loads[0].wait()
    for half in range(2):
        send_w(0, 1, half)
        send_w(0, 2, half)

    square = (SPANS, SPANS)
    places = order[...]
    diagonal = lax.broadcasted_iota(jnp.int32, square, 0) == lax.broadcasted_iota(jnp.int32, square, 1)
    column = jnp.sum(jnp.where(diagonal, jnp.broadcast_to(places, square), 0), axis=1, keepdims=True)
    slot_row = lax.broadcasted_iota(jnp.int32, (SPANS, TOK), 0)
    own_half = lax.broadcasted_iota(jnp.int32, (SPANS, TOK), 1) // SPAN
    own = slot_row == (z * NX + x) * 2 + own_half
    column = jnp.broadcast_to(column, (SPANS, TOK))
    place = jnp.sum(jnp.where(own, column, 0), axis=0, keepdims=True)
    mask = jnp.where(column >= place, HIDDEN, 0.0).astype(jnp.bfloat16)
    for n in (1, 2, 3):
        loads[n].wait()
    rot = qr[...].astype(jnp.float32).T.astype(jnp.bfloat16)
    for h in range(HEADS):
        cols = slice(h * TOK, (h + 1) * TOK)
        qaug[:LAT, cols] = nt_dot(wuk[:, cols], qn[:, cols]).astype(jnp.bfloat16)
        qaug[LAT : LAT + ROPE, cols] = rot[h * ROPE : (h + 1) * ROPE]
        qaug[LAT + ROPE :, cols] = mask

    def hand_on(n, a):
        here = group(n, a, 0)
        if a == 0:
            for s in (1, 3, 2):
                send(here, here, pair_of(w1_sem, n, s), along1(n, s))
        for s in (1, 3):
            send(here, here, pair_of(w2_sem, n, s, a), along2(n, s))

    def from_z(n):
        for d, place in PLACES.items():
            if d and place // 4 == n:
                arrived(kbuf.at[strip(d)], pair_of(z_sem, NZ - d), at(dz=d))
        hand_on(n, 0)

    def first_round(n):
        for a in (1, 3, 2):
            arrived(group(n, a, 0), pair_of(w1_sem, n, 4 - a), along1(n, a))
            hand_on(n, a)
        send(share(core, n, 0), share(core, n, 0), pair_of(p_sem, n, 0), partner)

    def come(n, b):
        for a in (0, 1, 3, 2):
            here = group(n, a, b)
            arrived(here, pair_of(w2_sem, n, 4 - b, a), along2(n, b))
            if (b, a) in ((1, 0), (1, 1), (3, 2), (3, 3)):
                send(here, here, pair_of(w2_sem, n, 2, a), along2(n, -b if b == 1 else 1))
        send(share(core, n, b), share(core, n, b), pair_of(p_sem, n, b), partner)

    def partner_has(n, b):
        arrived(share(other, n, b), pair_of(p_sem, n, b), partner)

    def attend(spots, lo, size, top, total):
        cols = slice(lo, lo + size)
        scores = [nn_dot(kbuf[spot, :], qaug[:, cols]) * FACTOR for spot in spots]
        for spot, score in zip(spots, scores):
            newest = jnp.maximum(top, jnp.max(score, axis=0, keepdims=True))
            shrink = jnp.exp2(top - newest)
            weight = jnp.exp2(score - newest)
            total = total * shrink + jnp.sum(weight.reshape(CHUNK // 8, 8, size), axis=0)
            acc[:, cols] = acc[:, cols] * shrink + tn_dot(kbuf[spot, :LAT], weight.astype(jnp.bfloat16))
            top = newest
        return top, total

    from_z(0)
    first_round(0)
    from_z(1)
    first_round(1)

    row = lax.broadcasted_iota(jnp.int32, (TOK, QUERIES), 0)
    col = lax.rem(lax.broadcasted_iota(jnp.int32, (TOK, QUERIES), 1), TOK)
    seen = (row <= col) & (row >= (col // SPAN) * SPAN)
    score = nn_dot(lat[...], qaug[:LAT, :]) + nn_dot(own_rope[...], qaug[LAT:, :])
    score = jnp.where(seen, score * FACTOR, HIDDEN)
    top = jnp.max(score, axis=0, keepdims=True)
    weight = jnp.exp2(score - top)
    total = jnp.sum(weight.reshape(TOK // 8, 8, QUERIES), axis=0)
    acc[...] = tn_dot(lat[...], weight.astype(jnp.bfloat16))
    loads[4].wait()
    wuv_t[...] = wuv[...].T

    WING = QUERIES // 2
    state = [(top[:, n * WING : (n + 1) * WING], total[:, n * WING : (n + 1) * WING]) for n in range(2)]

    def attend_all(n, b):
        partner_has(n, b)
        spot = chunk(n, b)
        for n in range(2):
            state[n] = attend([spot], n * WING, WING, *state[n])

    def serve(step, half):
        serve_w(2 * step - 1, half)
        serve_w(2 * step, half)

    serve(1, 0)
    attend_all(0, 0)
    come(0, 1)
    come(0, 3)
    attend_all(1, 0)
    come(1, 1)
    come(1, 3)
    serve(1, 1)
    attend_all(0, 1)
    come(0, 2)
    serve(2, 0)
    attend_all(0, 3)
    come(1, 2)
    attend_all(1, 1)
    serve(2, 1)
    attend_all(1, 3)
    attend_all(0, 2)
    serve(3, 0)
    partner_has(1, 2)

    for n in range(2):
        half = slice(n * WING, (n + 1) * WING)
        top, total = attend([chunk(1, 2)], n * WING, WING, *state[n])
        whole = jnp.sum(total, axis=0, keepdims=True)
        context = (acc[:, half] / whole).astype(jnp.bfloat16)
        for k in range(HEADS // 2):
            spot = slice((n * HEADS // 2 + k) * VDIM, (n * HEADS // 2 + k + 1) * VDIM)
            hog[x, spot] = nn_dot(wuv_t[spot, :], context[:, k * TOK : (k + 1) * TOK]).astype(jnp.bfloat16)
        for d in (1, 3):
            send(hog.at[x, half], hog.at[x, half], pair_of(a_sem, n, d), at(dx=d))
    serve(3, 1)

    def heads_from(n, o):
        here = hog.at[lax.rem(x + o, NX), n * WING : (n + 1) * WING]
        arrived(here, pair_of(a_sem, n, NX - o), at(dx=o))
        return here

    passed = heads_from(0, 1)
    send(passed, passed, pair_of(a_sem, 0, 2), at(dx=-1))
    passed = heads_from(1, 3)
    send(passed, passed, pair_of(a_sem, 1, 2), at(dx=1))
    for half in range(2):
        wait_w(7, half)

    tilt = 1 - 2 * lax.rem(z, 2)
    order_y = [lax.rem(z // 2 + NY + step, NY) for step in (0, -tilt, tilt, 2)]
    ahead = []

    def project(o):
        block = lax.rem(x + o, NX)
        for n in {1: (1,), 2: (0, 1), 3: (0,)}.get(o, ()):
            heads_from(n, o)
        for n, j in enumerate(order_y):
            c1s[o, n] = nn_dot(wbuf[2 * j + other], hog[block]).astype(jnp.bfloat16)
            send(c1s.at[o, n], c1r.at[o, n], pair_of(c1_sem, o, n), partner)
        for n, j in enumerate(order_y):
            kept = nn_dot(wbuf[2 * j + core], hog[block])
            arrived(c1r.at[o, n], pair_of(c1_sem, o, n), partner)
            c2s[o, n] = (kept + c1r[o, n].astype(jnp.float32)).astype(jnp.bfloat16)
            sems = (c2_sem.at[0, o, n], c2_sem.at[1, o, y])
            onward = copy(c2s.at[o, n], c2r.at[o, y], sems, (z, x, j, core))
            ahead.append((j, onward))

            @pl.when(j != y)
            def _():
                onward.start()

            @pl.when(j == y)
            def _():
                c2r[o, y] = c2s[o, n]

    def collect(o):
        for d in (1, 2, 3):
            yy = lax.rem(y + d, NY)
            arrived(c2r.at[o, yy], (c2_sem.at[0, o, 0], c2_sem.at[1, o, yy]), at(dy=d))
        summed = c2r[o, 0].astype(jnp.float32)
        for k in range(1, NY):
            summed = summed + c2r[o, k].astype(jnp.float32)
        if o:
            c3s[o] = summed.astype(jnp.bfloat16)
            send(c3s.at[o], c3r.at[x], pair_of(c3_sem, o), at(dx=o))
        else:
            c3r[x] = summed.astype(jnp.bfloat16)

    project(0)
    project(1)
    collect(0)
    project(3)
    collect(1)
    project(2)
    collect(3)
    collect(2)
    for d in (1, 2, 3):
        arrived(c3r.at[lax.rem(x + NX - d, NX)], pair_of(c3_sem, d), at(dx=-d))
    out[...] = c3r[...].reshape(NX * COLS, TOK).astype(jnp.float32).T.astype(jnp.bfloat16)

    for j, onward in ahead:

        @pl.when(j != y)
        def _():
            onward.wait_send()

    for made in sent:
        made.wait_send()


def local(q_nope, q_rope, latent, k_rope, span_order, w_uk, w_uv, w_o):
    bf16, f32 = jnp.bfloat16, jnp.float32
    dma = pltpu.SemaphoreType.DMA
    vmem = pl.BlockSpec(memory_space=pltpu.VMEM)
    anywhere = pl.BlockSpec(memory_space=pl.ANY)
    return pl.pallas_call(
        kernel,
        out_shape=jax.ShapeDtypeStruct((TOK, NX * COLS), bf16),
        in_specs=[vmem] * 3 + [anywhere] * 5,
        out_specs=vmem,
        scratch_shapes=[
            pltpu.VMEM((TOK, HEADS * NOPE), bf16),
            pltpu.VMEM((TOK, HEADS * ROPE), bf16),
            pltpu.VMEM((LAT, HEADS * NOPE), bf16),
            pltpu.VMEM((LAT, HEADS * VDIM), bf16),
            pltpu.VMEM((KEYS, WIDE), bf16),
            pltpu.VMEM((TOK, ROPE + SPANS), bf16),
            pltpu.VMEM((WIDE, QUERIES), bf16),
            pltpu.VMEM((LAT, QUERIES), f32),
            pltpu.VMEM((HEADS * VDIM, LAT), bf16),
            pltpu.VMEM((NZ, COLS, HEADS * VDIM), bf16),
            pltpu.VMEM((NX, HEADS * VDIM, TOK), bf16),
            pltpu.VMEM((NX, NY, COLS, TOK), bf16),
            pltpu.VMEM((NX, NY, COLS, TOK), bf16),
            pltpu.VMEM((NX, NY, COLS, TOK), bf16),
            pltpu.VMEM((NX, NY, COLS, TOK), bf16),
            pltpu.VMEM((NX, COLS, TOK), bf16),
            pltpu.VMEM((NX, COLS, TOK), bf16),
            dma((5,)),
            dma((2, NZ)),
            dma((2, 2, 4)),
            dma((2, 2, 4, 4)),
            dma((2, 2, 4)),
            dma((2, 2, NZ)),
            dma((2, 2, NX)),
            dma((2, NX, NY)),
            dma((2, NX, NY)),
            dma((2, NX)),
        ],
        compiler_params=pltpu.CompilerParams(
            collective_id=0, has_side_effects=True, vmem_limit_bytes=56 * 1024 * 1024
        ),
        cost_estimate=pl.CostEstimate(flops=11_000_000_000, bytes_accessed=4_000_000, transcendentals=4_200_000),
    )(latent, k_rope.T, span_order.reshape(1, -1), q_nope, q_rope, w_uk, w_uv, w_o.T)


def solution(mesh):
    torus = Mesh(mesh.devices.reshape(NZ, NX, NY, 2), ("z", "x", "y", "core"))
    ctx, head = ("z", "x"), ("y", "core")
    in_specs = (
        P(ctx, head),
        P(ctx, head),
        P(ctx, None),
        P(ctx, None),
        P(),
        P(None, head),
        P(None, head),
        P(head, ctx),
    )
    return jax.shard_map(local, mesh=torus, in_specs=in_specs, out_specs=P(ctx, head), check_vma=False)
```

```python
import math

import jax
import jax.numpy as jnp
from jax import lax
from jax.experimental import pallas as pl
from jax.experimental.pallas import tpu as pltpu
from jax.sharding import Mesh
from jax.sharding import PartitionSpec as P

NZ, NX, NY = 8, 4, 4
TOK, SPAN, SPANS = 128, 64, 64
HEADS, NOPE, ROPE, LAT, VDIM = 8, 128, 64, 512, 128
WIDE = LAT + ROPE + SPANS
QUERIES = HEADS * TOK
COLS = 224
KEYS = NZ * NX * TOK
STRIP = TOK // (2 * NY)
BUNDLE = NZ * STRIP
GROUP = BUNDLE // 2
PLACES = {0: 0, 1: 1, 7: 2, 2: 3, 6: 4, 3: 5, 5: 6, 4: 7}
CHUNK = 4 * BUNDLE
FACTOR = math.log2(math.e) / math.sqrt(NOPE + ROPE)
HIDDEN = -1e30
MESH = pl.DeviceIdType.MESH
DELTAS = (0, -1, 1, -2, 2, -3, 3, -4)


def nt_dot(a, b):
    return lax.dot_general(a, b, (((1,), (1,)), ((), ())), preferred_element_type=jnp.float32)


def tn_dot(a, b):
    return lax.dot_general(a, b, (((0,), (0,)), ((), ())), preferred_element_type=jnp.float32)


def nn_dot(a, b):
    return jnp.dot(a, b, preferred_element_type=jnp.float32)


def kernel(
    lat, kr, order, qn_in, qr_in, wuk_in, wuv_in, wo_in, out,
    qn, qr, wuk, wuv, kbuf, own_rope, qaug, acc, wuv_t, wbuf, hog, c1s, c1r, c2s, c2r, c3s, c3r,
    in_sem, z_sem, w1_sem, w2_sem, p_sem, o_sem, a_sem, c1_sem, c2_sem, c3_sem,
):
    z, x, y, core = (lax.axis_index(n) for n in ("z", "x", "y", "core"))
    other = 1 - core

    def at(dz=0, dx=0, dy=0):
        return (lax.rem(z + NZ + dz, NZ), lax.rem(x + NX + dx, NX), lax.rem(y + NY + dy, NY), core)

    partner = (z, x, y, other)
    peers = [partner] + [at(dz=d) for d in range(1, NZ)]
    peers += [at(dx=d) for d in (1, 2, 3)] + [at(dy=d) for d in (1, 2, 3)]
    barrier = pltpu.get_barrier_semaphore()
    for peer in peers:
        pl.semaphore_signal(barrier, inc=1, device_id=peer, device_id_type=MESH)

    loads = []
    for n, (src, dst) in enumerate(
        ((wo_in, wbuf.at[z]), (wuk_in, wuk), (qn_in, qn), (qr_in, qr), (wuv_in, wuv))
    ):
        loads.append(pltpu.make_async_copy(src, dst, in_sem.at[n]))
        loads[-1].start()

    sent = []

    def copy(src, dst, sems, device):
        return pltpu.make_async_remote_copy(
            src_ref=src, dst_ref=dst, send_sem=sems[0], recv_sem=sems[1], device_id=device, device_id_type=MESH
        )

    def send(src, dst, sems, device):
        made = copy(src, dst, sems, device)
        made.start()
        sent.append(made)

    def arrived(dst, sems, device):
        copy(dst, dst, sems, device).wait_recv()

    def pair_of(sems, *index):
        return sems.at[(0, *index)], sems.at[(1, *index)]

    def chunk_start(n, b):
        second = (x if n else y) + b + 4
        return (n * 4 + lax.rem(second, 4)) * CHUNK

    def chunk(n, b):
        return pl.ds(pl.multiple_of(chunk_start(n, b), CHUNK), CHUNK)

    def share(k, n, b):
        return kbuf.at[pl.ds(pl.multiple_of(chunk_start(n, b) + k * (CHUNK // 2), CHUNK // 2), CHUNK // 2)]

    def group_start(n, a, b):
        first = (y if n else x) + a + 4
        return chunk_start(n, b) + core * (CHUNK // 2) + lax.rem(first, 4) * GROUP

    def group(n, a, b):
        return kbuf.at[pl.ds(pl.multiple_of(group_start(n, a, b), GROUP), GROUP)]

    def along1(n, step):
        return at(dy=step) if n else at(dx=step)

    def along2(n, step):
        return at(dx=step) if n else at(dy=step)

    def strip(dz):
        place = PLACES[dz % NZ]
        start = group_start(place // 4, 0, 0) + place % 4 * STRIP
        return pl.ds(pl.multiple_of(start, STRIP), STRIP)

    own_rope[...] = jnp.zeros_like(own_rope)
    own_rope[:, :ROPE] = kr[...].astype(jnp.float32).T.astype(jnp.bfloat16)
    mine = pl.ds(pl.multiple_of((2 * y + core) * STRIP, STRIP), STRIP)
    own_slot = (z * NX + x) * 2 + y // 2
    lane = lax.broadcasted_iota(jnp.int32, (STRIP, ROPE + SPANS), 1)
    kbuf[strip(0), :LAT] = lat[mine, :]
    kbuf[strip(0), LAT:] = jnp.where(
        lane == ROPE + own_slot, 1.0, own_rope[mine, :].astype(jnp.float32)
    ).astype(jnp.bfloat16)

    tone = 1 - 2 * core
    ahead_z, behind_z = at(dz=tone), at(dz=-tone)

    def wpart(delta, half):
        zz = lax.rem(z + NZ + tone * delta, NZ)
        return wbuf.at[zz, pl.ds(half * (COLS // 2), COLS // 2)]

    def send_w(i, later, half):
        here = wpart(DELTAS[i], half)
        send(here, here, pair_of(o_sem, half, later), ahead_z if DELTAS[later] < 0 else behind_z)

    def wait_w(i, half):
        arrived(wpart(DELTAS[i], half), pair_of(o_sem, half, i), ahead_z if DELTAS[i] > 0 else behind_z)

    def serve_w(i, half):
        wait_w(i, half)
        if i + 2 < NZ:
            send_w(i, i + 2, half)

    square = (SPANS, SPANS)
    places = order[...]
    diagonal = lax.broadcasted_iota(jnp.int32, square, 0) == lax.broadcasted_iota(jnp.int32, square, 1)
    column = jnp.sum(jnp.where(diagonal, jnp.broadcast_to(places, square), 0), axis=1, keepdims=True)
    slot_row = lax.broadcasted_iota(jnp.int32, (SPANS, TOK), 0)
    own_half = lax.broadcasted_iota(jnp.int32, (SPANS, TOK), 1) // SPAN
    own = slot_row == (z * NX + x) * 2 + own_half
    column = jnp.broadcast_to(column, (SPANS, TOK))
    place = jnp.sum(jnp.where(own, column, 0), axis=0, keepdims=True)
    mask = jnp.where(column >= place, HIDDEN, 0.0).astype(jnp.bfloat16)
    for n in (1, 2, 3):
        loads[n].wait()
    rot = qr[...].astype(jnp.float32).T.astype(jnp.bfloat16)
    for h in range(HEADS):
        cols = slice(h * TOK, (h + 1) * TOK)
        qaug[:LAT, cols] = nt_dot(wuk[:, cols], qn[:, cols]).astype(jnp.bfloat16)
        qaug[LAT : LAT + ROPE, cols] = rot[h * ROPE : (h + 1) * ROPE]
        qaug[LAT + ROPE :, cols] = mask

    pl.semaphore_wait(barrier, len(peers))

    for d in (6, 7, 1, 2, 4, 5, 3):
        send(kbuf.at[strip(0)], kbuf.at[strip(-d)], pair_of(z_sem, d), at(dz=d))

    loads[0].wait()
    for half in range(2):
        for later in (1, 2):
            send_w(0, later, half)

    row = lax.broadcasted_iota(jnp.int32, (TOK, QUERIES), 0)
    col = lax.rem(lax.broadcasted_iota(jnp.int32, (TOK, QUERIES), 1), TOK)
    seen = (row <= col) & (row >= (col // SPAN) * SPAN)
    score = nn_dot(lat[...], qaug[:LAT, :]) + nn_dot(own_rope[...], qaug[LAT:, :])
    score = jnp.where(seen, score * FACTOR, HIDDEN)
    top = jnp.max(score, axis=0, keepdims=True)
    weight = jnp.exp2(score - top)
    total = jnp.sum(weight.reshape(TOK // 8, 8, QUERIES), axis=0)
    acc[...] = tn_dot(lat[...], weight.astype(jnp.bfloat16))
    loads[4].wait()
    wuv_t[...] = wuv[...].T

    def hand_on(n, a):
        here = group(n, a, 0)
        if a == 0:
            for s in (1, 3, 2):
                send(here, here, pair_of(w1_sem, n, s), along1(n, s))
        for s in (1, 3):
            send(here, here, pair_of(w2_sem, n, s, a), along2(n, s))

    def from_z(n):
        for d, place in PLACES.items():
            if d and place // 4 == n:
                arrived(kbuf.at[strip(d)], pair_of(z_sem, NZ - d), at(dz=d))
        hand_on(n, 0)

    def first_round(n):
        for a in (1, 3, 2):
            arrived(group(n, a, 0), pair_of(w1_sem, n, 4 - a), along1(n, a))
            hand_on(n, a)
        send(share(core, n, 0), share(core, n, 0), pair_of(p_sem, n, 0), partner)

    def come(n, b):
        for a in (0, 1, 3, 2):
            here = group(n, a, b)
            arrived(here, pair_of(w2_sem, n, 4 - b, a), along2(n, b))
            if (b, a) in ((1, 0), (1, 1), (3, 2), (3, 3)):
                send(here, here, pair_of(w2_sem, n, 2, a), along2(n, -b if b == 1 else 1))
        send(share(core, n, b), share(core, n, b), pair_of(p_sem, n, b), partner)

    def partner_has(n, b):
        arrived(share(other, n, b), pair_of(p_sem, n, b), partner)

    def attend(spots, lo, size, top, total):
        cols = slice(lo, lo + size)
        scores = [nn_dot(kbuf[spot, :], qaug[:, cols]) * FACTOR for spot in spots]
        for spot, score in zip(spots, scores):
            newest = jnp.maximum(top, jnp.max(score, axis=0, keepdims=True))
            shrink = jnp.exp2(top - newest)
            weight = jnp.exp2(score - newest)
            total = total * shrink + jnp.sum(weight.reshape(CHUNK // 8, 8, size), axis=0)
            acc[:, cols] = acc[:, cols] * shrink + tn_dot(kbuf[spot, :LAT], weight.astype(jnp.bfloat16))
            top = newest
        return top, total

    from_z(0)
    first_round(0)
    from_z(1)
    first_round(1)

    WING = QUERIES // 2
    state = [(top[:, n * WING : (n + 1) * WING], total[:, n * WING : (n + 1) * WING]) for n in range(2)]

    def attend_all(n, b):
        partner_has(n, b)
        spot = chunk(n, b)
        for n in range(2):
            state[n] = attend([spot], n * WING, WING, *state[n])

    def serve(step, half):
        serve_w(2 * step - 1, half)
        serve_w(2 * step, half)

    serve(1, 0)
    attend_all(0, 0)
    serve(1, 1)
    come(0, 1)
    come(0, 3)
    attend_all(1, 0)
    serve(2, 0)
    come(1, 1)
    come(1, 3)
    serve(2, 1)
    attend_all(0, 1)
    come(0, 2)
    serve(3, 0)
    attend_all(0, 3)
    come(1, 2)
    attend_all(1, 1)
    serve(3, 1)
    attend_all(1, 3)
    attend_all(0, 2)
    partner_has(1, 2)

    for n in range(2):
        half = slice(n * WING, (n + 1) * WING)
        top, total = attend([chunk(1, 2)], n * WING, WING, *state[n])
        whole = jnp.sum(total, axis=0, keepdims=True)
        context = (acc[:, half] / whole).astype(jnp.bfloat16)
        for k in range(HEADS // 2):
            spot = slice((n * HEADS // 2 + k) * VDIM, (n * HEADS // 2 + k + 1) * VDIM)
            hog[x, spot] = nn_dot(wuv_t[spot, :], context[:, k * TOK : (k + 1) * TOK]).astype(jnp.bfloat16)
        for d in (1, 3):
            send(hog.at[x, half], hog.at[x, half], pair_of(a_sem, n, d), at(dx=d))

    def heads_from(n, o):
        here = hog.at[lax.rem(x + o, NX), n * WING : (n + 1) * WING]
        arrived(here, pair_of(a_sem, n, NX - o), at(dx=o))
        return here

    early = list(sent)
    sent.clear()

    passed = heads_from(0, 1)
    send(passed, passed, pair_of(a_sem, 0, 2), at(dx=-1))
    for made in early:
        made.wait_send()
    for half in range(2):
        wait_w(7, half)

    tilt = 1 - 2 * lax.rem(z, 2)
    order_y = [lax.rem(z // 2 + NY + step, NY) for step in (0, -tilt, tilt, 2)]
    ahead = []

    def project(*steps):
        right = jnp.concatenate([hog[lax.rem(x + o, NX)] for o in steps], axis=1)
        parts = [(o, slice(i * TOK, (i + 1) * TOK)) for i, o in enumerate(steps)]
        for n, j in enumerate(order_y):
            given = nn_dot(wbuf[2 * j + other], right).astype(jnp.bfloat16)
            for o, part in parts:
                c1s[o, n] = given[:, part]
                send(c1s.at[o, n], c1r.at[o, n], pair_of(c1_sem, o, n), partner)
        for n, j in enumerate(order_y):
            kept = nn_dot(wbuf[2 * j + core], right)
            for o, part in parts:
                arrived(c1r.at[o, n], pair_of(c1_sem, o, n), partner)
                c2s[o, n] = (kept[:, part] + c1r[o, n].astype(jnp.float32)).astype(jnp.bfloat16)
                sems = (c2_sem.at[0, o, n], c2_sem.at[1, o, y])
                onward = copy(c2s.at[o, n], c2r.at[o, y], sems, (z, x, j, core))
                ahead.append((j, onward))

                @pl.when(j != y)
                def _():
                    onward.start()

                @pl.when(j == y)
                def _():
                    c2r[o, y] = c2s[o, n]

    def collect(o):
        for d in (1, 2, 3):
            yy = lax.rem(y + d, NY)
            arrived(c2r.at[o, yy], (c2_sem.at[0, o, 0], c2_sem.at[1, o, yy]), at(dy=d))
        summed = c2r[o, 0].astype(jnp.float32)
        for k in range(1, NY):
            summed = summed + c2r[o, k].astype(jnp.float32)
        if o:
            c3s[o] = summed.astype(jnp.bfloat16)
            send(c3s.at[o], c3r.at[x], pair_of(c3_sem, o), at(dx=o))
        else:
            c3r[x] = summed.astype(jnp.bfloat16)

    project(0)
    passed = heads_from(1, 3)
    send(passed, passed, pair_of(a_sem, 1, 2), at(dx=1))
    heads_from(1, 1)
    heads_from(0, 3)
    project(1, 3)
    collect(0)
    heads_from(0, 2)
    heads_from(1, 2)
    project(2)
    collect(1)
    collect(3)
    collect(2)
    for d in (1, 2, 3):
        arrived(c3r.at[lax.rem(x + NX - d, NX)], pair_of(c3_sem, d), at(dx=-d))
    out[...] = c3r[...].reshape(NX * COLS, TOK).astype(jnp.float32).T.astype(jnp.bfloat16)

    for j, onward in ahead:

        @pl.when(j != y)
        def _():
            onward.wait_send()

    for made in sent:
        made.wait_send()


def local(q_nope, q_rope, latent, k_rope, span_order, w_uk, w_uv, w_o):
    bf16, f32 = jnp.bfloat16, jnp.float32
    dma = pltpu.SemaphoreType.DMA
    vmem = pl.BlockSpec(memory_space=pltpu.VMEM)
    anywhere = pl.BlockSpec(memory_space=pl.ANY)
    return pl.pallas_call(
        kernel,
        out_shape=jax.ShapeDtypeStruct((TOK, NX * COLS), bf16),
        in_specs=[vmem] * 3 + [anywhere] * 5,
        out_specs=vmem,
        scratch_shapes=[
            pltpu.VMEM((TOK, HEADS * NOPE), bf16),
            pltpu.VMEM((TOK, HEADS * ROPE), bf16),
            pltpu.VMEM((LAT, HEADS * NOPE), bf16),
            pltpu.VMEM((LAT, HEADS * VDIM), bf16),
            pltpu.VMEM((KEYS, WIDE), bf16),
            pltpu.VMEM((TOK, ROPE + SPANS), bf16),
            pltpu.VMEM((WIDE, QUERIES), bf16),
            pltpu.VMEM((LAT, QUERIES), f32),
            pltpu.VMEM((HEADS * VDIM, LAT), bf16),
            pltpu.VMEM((NZ, COLS, HEADS * VDIM), bf16),
            pltpu.VMEM((NX, HEADS * VDIM, TOK), bf16),
            pltpu.VMEM((NX, NY, COLS, TOK), bf16),
            pltpu.VMEM((NX, NY, COLS, TOK), bf16),
            pltpu.VMEM((NX, NY, COLS, TOK), bf16),
            pltpu.VMEM((NX, NY, COLS, TOK), bf16),
            pltpu.VMEM((NX, COLS, TOK), bf16),
            pltpu.VMEM((NX, COLS, TOK), bf16),
            dma((5,)),
            dma((2, NZ)),
            dma((2, 2, 4)),
            dma((2, 2, 4, 4)),
            dma((2, 2, 4)),
            dma((2, 2, NZ)),
            dma((2, 2, NX)),
            dma((2, NX, NY)),
            dma((2, NX, NY)),
            dma((2, NX)),
        ],
        compiler_params=pltpu.CompilerParams(
            collective_id=0, has_side_effects=True, vmem_limit_bytes=56 * 1024 * 1024
        ),
        cost_estimate=pl.CostEstimate(flops=11_000_000_000, bytes_accessed=4_000_000, transcendentals=4_200_000),
    )(latent, k_rope.T, span_order.reshape(1, -1), q_nope, q_rope, w_uk, w_uv, w_o.T)


def solution(mesh):
    torus = Mesh(mesh.devices.reshape(NZ, NX, NY, 2), ("z", "x", "y", "core"))
    ctx, head = ("z", "x"), ("y", "core")
    in_specs = (
        P(ctx, head),
        P(ctx, head),
        P(ctx, None),
        P(ctx, None),
        P(),
        P(None, head),
        P(None, head),
        P(head, ctx),
    )
    return jax.shard_map(local, mesh=torus, in_specs=in_specs, out_specs=P(ctx, head), check_vma=False)
```

```python
import math

import jax
import jax.numpy as jnp
from jax import lax
from jax.experimental import pallas as pl
from jax.experimental.pallas import tpu as pltpu
from jax.sharding import Mesh
from jax.sharding import PartitionSpec as P

NZ, NX, NY = 8, 4, 4
TOK, SPAN, SPANS = 128, 64, 64
HEADS, NOPE, ROPE, LAT, VDIM = 8, 128, 64, 512, 128
WIDE = LAT + ROPE + SPANS
QUERIES = HEADS * TOK
COLS = 224
KEYS = NZ * NX * TOK
STRIP = TOK // (2 * NY)
BUNDLE = NZ * STRIP
GROUP = BUNDLE // 2
PLACES = {0: 0, 1: 1, 7: 2, 2: 3, 6: 4, 3: 5, 5: 6, 4: 7}
CHUNK = 4 * BUNDLE
FACTOR = math.log2(math.e) / math.sqrt(NOPE + ROPE)
HIDDEN = -1e30
MESH = pl.DeviceIdType.MESH
DELTAS = (0, -1, 1, -2, 2, -3, 3, -4)


def nt_dot(a, b):
    return lax.dot_general(a, b, (((1,), (1,)), ((), ())), preferred_element_type=jnp.float32)


def tn_dot(a, b):
    return lax.dot_general(a, b, (((0,), (0,)), ((), ())), preferred_element_type=jnp.float32)


def nn_dot(a, b):
    return jnp.dot(a, b, preferred_element_type=jnp.float32)


def kernel(
    lat, kr, order, qn_in, qr_in, wuk_in, wuv_in, wo_in, out,
    qn, qr, wuk, wuv, kbuf, own_rope, qaug, acc, wuv_t, wbuf, hog, c1s, c1r, c2s, c2r, c3s, c3r,
    in_sem, z_sem, w1_sem, w2_sem, p_sem, o_sem, a_sem, c1_sem, c2_sem, c3_sem,
):
    z, x, y, core = (lax.axis_index(n) for n in ("z", "x", "y", "core"))
    other = 1 - core

    def at(dz=0, dx=0, dy=0):
        return (lax.rem(z + NZ + dz, NZ), lax.rem(x + NX + dx, NX), lax.rem(y + NY + dy, NY), core)

    partner = (z, x, y, other)
    peers = [partner] + [at(dz=d) for d in range(1, NZ)]
    peers += [at(dx=d) for d in (1, 2, 3)] + [at(dy=d) for d in (1, 2, 3)]
    barrier = pltpu.get_barrier_semaphore()
    for peer in peers:
        pl.semaphore_signal(barrier, inc=1, device_id=peer, device_id_type=MESH)

    loads = []
    for n, (src, dst) in enumerate(
        ((wo_in, wbuf.at[z]), (wuk_in, wuk), (qn_in, qn), (qr_in, qr), (wuv_in, wuv))
    ):
        loads.append(pltpu.make_async_copy(src, dst, in_sem.at[n]))
        loads[-1].start()

    sent = []

    def copy(src, dst, sems, device):
        return pltpu.make_async_remote_copy(
            src_ref=src, dst_ref=dst, send_sem=sems[0], recv_sem=sems[1], device_id=device, device_id_type=MESH
        )

    def send(src, dst, sems, device):
        made = copy(src, dst, sems, device)
        made.start()
        sent.append(made)

    def arrived(dst, sems, device):
        copy(dst, dst, sems, device).wait_recv()

    def pair_of(sems, *index):
        return sems.at[(0, *index)], sems.at[(1, *index)]

    def chunk_start(n, b):
        second = (x if n else y) + b + 4
        return (n * 4 + lax.rem(second, 4)) * CHUNK

    def chunk(n, b):
        return pl.ds(pl.multiple_of(chunk_start(n, b), CHUNK), CHUNK)

    def share(k, n, b):
        return kbuf.at[pl.ds(pl.multiple_of(chunk_start(n, b) + k * (CHUNK // 2), CHUNK // 2), CHUNK // 2)]

    def group_start(n, a, b):
        first = (y if n else x) + a + 4
        return chunk_start(n, b) + core * (CHUNK // 2) + lax.rem(first, 4) * GROUP

    def group(n, a, b):
        return kbuf.at[pl.ds(pl.multiple_of(group_start(n, a, b), GROUP), GROUP)]

    def along1(n, step):
        return at(dy=step) if n else at(dx=step)

    def along2(n, step):
        return at(dx=step) if n else at(dy=step)

    def strip(dz):
        place = PLACES[dz % NZ]
        start = group_start(place // 4, 0, 0) + place % 4 * STRIP
        return pl.ds(pl.multiple_of(start, STRIP), STRIP)

    own_rope[...] = jnp.zeros_like(own_rope)
    own_rope[:, :ROPE] = kr[...].astype(jnp.float32).T.astype(jnp.bfloat16)
    mine = pl.ds(pl.multiple_of((2 * y + core) * STRIP, STRIP), STRIP)
    own_slot = (z * NX + x) * 2 + y // 2
    lane = lax.broadcasted_iota(jnp.int32, (STRIP, ROPE + SPANS), 1)
    kbuf[strip(0), :LAT] = lat[mine, :]
    kbuf[strip(0), LAT:] = jnp.where(
        lane == ROPE + own_slot, 1.0, own_rope[mine, :].astype(jnp.float32)
    ).astype(jnp.bfloat16)

    pl.semaphore_wait(barrier, len(peers))

    for d in (6, 7, 1, 2, 4, 5, 3):
        send(kbuf.at[strip(0)], kbuf.at[strip(-d)], pair_of(z_sem, d), at(dz=d))

    tone = 1 - 2 * core
    ahead_z, behind_z = at(dz=tone), at(dz=-tone)

    def wpart(delta, half):
        zz = lax.rem(z + NZ + tone * delta, NZ)
        return wbuf.at[zz, pl.ds(half * (COLS // 2), COLS // 2)]

    def send_w(i, later, half):
        here = wpart(DELTAS[i], half)
        send(here, here, pair_of(o_sem, half, later), ahead_z if DELTAS[later] < 0 else behind_z)

    def wait_w(i, half):
        arrived(wpart(DELTAS[i], half), pair_of(o_sem, half, i), ahead_z if DELTAS[i] > 0 else behind_z)

    def serve_w(i, half):
        wait_w(i, half)
        if i + 2 < NZ:
            send_w(i, i + 2, half)

    loads[0].wait()
    for half in range(2):
        send_w(0, 1, half)
        send_w(0, 2, half)

    square = (SPANS, SPANS)
    places = order[...]
    diagonal = lax.broadcasted_iota(jnp.int32, square, 0) == lax.broadcasted_iota(jnp.int32, square, 1)
    column = jnp.sum(jnp.where(diagonal, jnp.broadcast_to(places, square), 0), axis=1, keepdims=True)
    slot_row = lax.broadcasted_iota(jnp.int32, (SPANS, TOK), 0)
    own_half = lax.broadcasted_iota(jnp.int32, (SPANS, TOK), 1) // SPAN
    own = slot_row == (z * NX + x) * 2 + own_half
    column = jnp.broadcast_to(column, (SPANS, TOK))
    place = jnp.sum(jnp.where(own, column, 0), axis=0, keepdims=True)
    mask = jnp.where(column >= place, HIDDEN, 0.0).astype(jnp.bfloat16)
    for n in (1, 2, 3):
        loads[n].wait()
    rot = qr[...].astype(jnp.float32).T.astype(jnp.bfloat16)
    for h in range(HEADS):
        cols = slice(h * TOK, (h + 1) * TOK)
        qaug[:LAT, cols] = nt_dot(wuk[:, cols], qn[:, cols]).astype(jnp.bfloat16)
        qaug[LAT : LAT + ROPE, cols] = rot[h * ROPE : (h + 1) * ROPE]
        qaug[LAT + ROPE :, cols] = mask

    def hand_on(n, a):
        here = group(n, a, 0)
        if a == 0:
            for s in (1, 3, 2):
                send(here, here, pair_of(w1_sem, n, s), along1(n, s))
        for s in (1, 3):
            send(here, here, pair_of(w2_sem, n, s, a), along2(n, s))

    def from_z(n):
        for d, place in PLACES.items():
            if d and place // 4 == n:
                arrived(kbuf.at[strip(d)], pair_of(z_sem, NZ - d), at(dz=d))
        hand_on(n, 0)

    def first_round(n):
        for a in (1, 3, 2):
            arrived(group(n, a, 0), pair_of(w1_sem, n, 4 - a), along1(n, a))
            hand_on(n, a)
        send(share(core, n, 0), share(core, n, 0), pair_of(p_sem, n, 0), partner)

    def come(n, b):
        for a in (0, 1, 3, 2):
            here = group(n, a, b)
            arrived(here, pair_of(w2_sem, n, 4 - b, a), along2(n, b))
            if (b, a) in ((1, 0), (1, 1), (3, 2), (3, 3)):
                send(here, here, pair_of(w2_sem, n, 2, a), along2(n, -b if b == 1 else 1))
        send(share(core, n, b), share(core, n, b), pair_of(p_sem, n, b), partner)

    def partner_has(n, b):
        arrived(share(other, n, b), pair_of(p_sem, n, b), partner)

    def attend(spots, lo, size, top, total):
        cols = slice(lo, lo + size)
        scores = [nn_dot(kbuf[spot, :], qaug[:, cols]) * FACTOR for spot in spots]
        for spot, score in zip(spots, scores):
            newest = jnp.maximum(top, jnp.max(score, axis=0, keepdims=True))
            shrink = jnp.exp2(top - newest)
            weight = jnp.exp2(score - newest)
            total = total * shrink + jnp.sum(weight.reshape(CHUNK // 8, 8, size), axis=0)
            acc[:, cols] = acc[:, cols] * shrink + tn_dot(kbuf[spot, :LAT], weight.astype(jnp.bfloat16))
            top = newest
        return top, total

    from_z(0)
    first_round(0)
    from_z(1)
    first_round(1)

    row = lax.broadcasted_iota(jnp.int32, (TOK, QUERIES), 0)
    col = lax.rem(lax.broadcasted_iota(jnp.int32, (TOK, QUERIES), 1), TOK)
    seen = (row <= col) & (row >= (col // SPAN) * SPAN)
    score = nn_dot(lat[...], qaug[:LAT, :]) + nn_dot(own_rope[...], qaug[LAT:, :])
    score = jnp.where(seen, score * FACTOR, HIDDEN)
    top = jnp.max(score, axis=0, keepdims=True)
    weight = jnp.exp2(score - top)
    total = jnp.sum(weight.reshape(TOK // 8, 8, QUERIES), axis=0)
    acc[...] = tn_dot(lat[...], weight.astype(jnp.bfloat16))
    loads[4].wait()
    wuv_t[...] = wuv[...].T

    WING = QUERIES // 2
    state = [(top[:, n * WING : (n + 1) * WING], total[:, n * WING : (n + 1) * WING]) for n in range(2)]

    def attend_all(n, b):
        partner_has(n, b)
        spot = chunk(n, b)
        for n in range(2):
            state[n] = attend([spot], n * WING, WING, *state[n])

    def serve(step, half):
        serve_w(2 * step - 1, half)
        serve_w(2 * step, half)

    serve(1, 0)
    attend_all(0, 0)
    come(0, 1)
    come(0, 3)
    attend_all(1, 0)
    come(1, 1)
    come(1, 3)
    serve(1, 1)
    attend_all(0, 1)
    come(0, 2)
    serve(2, 0)
    attend_all(0, 3)
    come(1, 2)
    attend_all(1, 1)
    serve(2, 1)
    attend_all(1, 3)
    attend_all(0, 2)
    serve(3, 0)
    partner_has(1, 2)

    for n in range(2):
        half = slice(n * WING, (n + 1) * WING)
        top, total = attend([chunk(1, 2)], n * WING, WING, *state[n])
        whole = jnp.sum(total, axis=0, keepdims=True)
        context = (acc[:, half] / whole).astype(jnp.bfloat16)
        for k in range(HEADS // 2):
            spot = slice((n * HEADS // 2 + k) * VDIM, (n * HEADS // 2 + k + 1) * VDIM)
            hog[x, spot] = nn_dot(wuv_t[spot, :], context[:, k * TOK : (k + 1) * TOK]).astype(jnp.bfloat16)
        for d in (1, 3):
            send(hog.at[x, half], hog.at[x, half], pair_of(a_sem, n, d), at(dx=d))
    serve(3, 1)

    def heads_from(n, o):
        here = hog.at[lax.rem(x + o, NX), n * WING : (n + 1) * WING]
        arrived(here, pair_of(a_sem, n, NX - o), at(dx=o))
        return here

    passed = heads_from(0, 1)
    send(passed, passed, pair_of(a_sem, 0, 2), at(dx=-1))
    passed = heads_from(1, 3)
    send(passed, passed, pair_of(a_sem, 1, 2), at(dx=1))
    for half in range(2):
        wait_w(7, half)

    tilt = 1 - 2 * lax.rem(z, 2)
    order_y = [lax.rem(z // 2 + NY + step, NY) for step in (0, -tilt, tilt, 2)]
    ahead = []

    def project(*steps):
        right = jnp.concatenate([hog[lax.rem(x + o, NX)] for o in steps], axis=1)
        parts = [(o, slice(i * TOK, (i + 1) * TOK)) for i, o in enumerate(steps)]
        for n, j in enumerate(order_y):
            given = nn_dot(wbuf[2 * j + other], right).astype(jnp.bfloat16)
            for o, part in parts:
                c1s[o, n] = given[:, part]
                send(c1s.at[o, n], c1r.at[o, n], pair_of(c1_sem, o, n), partner)
        for n, j in enumerate(order_y):
            kept = nn_dot(wbuf[2 * j + core], right)
            for o, part in parts:
                arrived(c1r.at[o, n], pair_of(c1_sem, o, n), partner)
                c2s[o, n] = (kept[:, part] + c1r[o, n].astype(jnp.float32)).astype(jnp.bfloat16)
                sems = (c2_sem.at[0, o, n], c2_sem.at[1, o, y])
                onward = copy(c2s.at[o, n], c2r.at[o, y], sems, (z, x, j, core))
                ahead.append((j, onward))

                @pl.when(j != y)
                def _():
                    onward.start()

                @pl.when(j == y)
                def _():
                    c2r[o, y] = c2s[o, n]

    def collect(o):
        for d in (1, 2, 3):
            yy = lax.rem(y + d, NY)
            arrived(c2r.at[o, yy], (c2_sem.at[0, o, 0], c2_sem.at[1, o, yy]), at(dy=d))
        summed = c2r[o, 0].astype(jnp.float32)
        for k in range(1, NY):
            summed = summed + c2r[o, k].astype(jnp.float32)
        if o:
            c3s[o] = summed.astype(jnp.bfloat16)
            send(c3s.at[o], c3r.at[x], pair_of(c3_sem, o), at(dx=o))
        else:
            c3r[x] = summed.astype(jnp.bfloat16)

    project(0)
    heads_from(1, 1)
    heads_from(0, 3)
    project(1, 3)
    collect(0)
    heads_from(0, 2)
    heads_from(1, 2)
    project(2)
    collect(1)
    collect(3)
    collect(2)
    for d in (1, 2, 3):
        arrived(c3r.at[lax.rem(x + NX - d, NX)], pair_of(c3_sem, d), at(dx=-d))
    out[...] = c3r[...].reshape(NX * COLS, TOK).astype(jnp.float32).T.astype(jnp.bfloat16)

    for j, onward in ahead:

        @pl.when(j != y)
        def _():
            onward.wait_send()

    for made in sent:
        made.wait_send()


def local(q_nope, q_rope, latent, k_rope, span_order, w_uk, w_uv, w_o):
    bf16, f32 = jnp.bfloat16, jnp.float32
    dma = pltpu.SemaphoreType.DMA
    vmem = pl.BlockSpec(memory_space=pltpu.VMEM)
    anywhere = pl.BlockSpec(memory_space=pl.ANY)
    return pl.pallas_call(
        kernel,
        out_shape=jax.ShapeDtypeStruct((TOK, NX * COLS), bf16),
        in_specs=[vmem] * 3 + [anywhere] * 5,
        out_specs=vmem,
        scratch_shapes=[
            pltpu.VMEM((TOK, HEADS * NOPE), bf16),
            pltpu.VMEM((TOK, HEADS * ROPE), bf16),
            pltpu.VMEM((LAT, HEADS * NOPE), bf16),
            pltpu.VMEM((LAT, HEADS * VDIM), bf16),
            pltpu.VMEM((KEYS, WIDE), bf16),
            pltpu.VMEM((TOK, ROPE + SPANS), bf16),
            pltpu.VMEM((WIDE, QUERIES), bf16),
            pltpu.VMEM((LAT, QUERIES), f32),
            pltpu.VMEM((HEADS * VDIM, LAT), bf16),
            pltpu.VMEM((NZ, COLS, HEADS * VDIM), bf16),
            pltpu.VMEM((NX, HEADS * VDIM, TOK), bf16),
            pltpu.VMEM((NX, NY, COLS, TOK), bf16),
            pltpu.VMEM((NX, NY, COLS, TOK), bf16),
            pltpu.VMEM((NX, NY, COLS, TOK), bf16),
            pltpu.VMEM((NX, NY, COLS, TOK), bf16),
            pltpu.VMEM((NX, COLS, TOK), bf16),
            pltpu.VMEM((NX, COLS, TOK), bf16),
            dma((5,)),
            dma((2, NZ)),
            dma((2, 2, 4)),
            dma((2, 2, 4, 4)),
            dma((2, 2, 4)),
            dma((2, 2, NZ)),
            dma((2, 2, NX)),
            dma((2, NX, NY)),
            dma((2, NX, NY)),
            dma((2, NX)),
        ],
        compiler_params=pltpu.CompilerParams(
            collective_id=0, has_side_effects=True, vmem_limit_bytes=56 * 1024 * 1024
        ),
        cost_estimate=pl.CostEstimate(flops=11_000_000_000, bytes_accessed=4_000_000, transcendentals=4_200_000),
    )(latent, k_rope.T, span_order.reshape(1, -1), q_nope, q_rope, w_uk, w_uv, w_o.T)


def solution(mesh):
    torus = Mesh(mesh.devices.reshape(NZ, NX, NY, 2), ("z", "x", "y", "core"))
    ctx, head = ("z", "x"), ("y", "core")
    in_specs = (
        P(ctx, head),
        P(ctx, head),
        P(ctx, None),
        P(ctx, None),
        P(),
        P(None, head),
        P(None, head),
        P(head, ctx),
    )
    return jax.shard_map(local, mesh=torus, in_specs=in_specs, out_specs=P(ctx, head), check_vma=False)
```

```python
import math

import jax
import jax.numpy as jnp
from jax import lax
from jax.experimental import pallas as pl
from jax.experimental.pallas import tpu as pltpu
from jax.sharding import Mesh
from jax.sharding import PartitionSpec as P

NZ, NX, NY = 8, 4, 4
TOK, SPAN, SPANS = 128, 64, 64
HEADS, NOPE, ROPE, LAT, VDIM = 8, 128, 64, 512, 128
WIDE = LAT + ROPE + SPANS
QUERIES = HEADS * TOK
COLS = 224
KEYS = NZ * NX * TOK
STRIP = TOK // (2 * NY)
BUNDLE = NZ * STRIP
GROUP = BUNDLE // 2
PLACES = {0: 0, 1: 1, 7: 2, 2: 3, 6: 4, 3: 5, 5: 6, 4: 7}
CHUNK = 4 * BUNDLE
FACTOR = math.log2(math.e) / math.sqrt(NOPE + ROPE)
HIDDEN = -1e30
MESH = pl.DeviceIdType.MESH
DELTAS = (0, -1, 1, -2, 2, -3, 3, -4)


def nt_dot(a, b):
    return lax.dot_general(a, b, (((1,), (1,)), ((), ())), preferred_element_type=jnp.float32)


def tn_dot(a, b):
    return lax.dot_general(a, b, (((0,), (0,)), ((), ())), preferred_element_type=jnp.float32)


def nn_dot(a, b):
    return jnp.dot(a, b, preferred_element_type=jnp.float32)


def kernel(
    lat, kr, order, qn_in, qr_in, wuk_in, wuv_in, wo_in, out,
    qn, qr, wuk, wuv, kbuf, own_rope, qaug, acc, wuv_t, wbuf, hog, c1s, c1r, c2s, c2r, c3s, c3r,
    in_sem, z_sem, w1_sem, w2_sem, p_sem, o_sem, a_sem, c1_sem, c2_sem, c3_sem,
):
    z, x, y, core = (lax.axis_index(n) for n in ("z", "x", "y", "core"))
    other = 1 - core

    def at(dz=0, dx=0, dy=0):
        return (lax.rem(z + NZ + dz, NZ), lax.rem(x + NX + dx, NX), lax.rem(y + NY + dy, NY), core)

    partner = (z, x, y, other)
    peers = [partner] + [at(dz=d) for d in range(1, NZ)]
    peers += [at(dx=d) for d in (1, 2, 3)] + [at(dy=d) for d in (1, 2, 3)]
    barrier = pltpu.get_barrier_semaphore()
    for peer in peers:
        pl.semaphore_signal(barrier, inc=1, device_id=peer, device_id_type=MESH)

    loads = []
    for n, (src, dst) in enumerate(
        ((wo_in, wbuf.at[z]), (wuk_in, wuk), (qn_in, qn), (qr_in, qr), (wuv_in, wuv))
    ):
        loads.append(pltpu.make_async_copy(src, dst, in_sem.at[n]))
        loads[-1].start()

    sent = []

    def copy(src, dst, sems, device):
        return pltpu.make_async_remote_copy(
            src_ref=src, dst_ref=dst, send_sem=sems[0], recv_sem=sems[1], device_id=device, device_id_type=MESH
        )

    def send(src, dst, sems, device):
        made = copy(src, dst, sems, device)
        made.start()
        sent.append(made)

    def arrived(dst, sems, device):
        copy(dst, dst, sems, device).wait_recv()

    def pair_of(sems, *index):
        return sems.at[(0, *index)], sems.at[(1, *index)]

    def chunk_start(n, b):
        second = (x if n else y) + b + 4
        return (n * 4 + lax.rem(second, 4)) * CHUNK

    def chunk(n, b):
        return pl.ds(pl.multiple_of(chunk_start(n, b), CHUNK), CHUNK)

    def share(k, n, b):
        return kbuf.at[pl.ds(pl.multiple_of(chunk_start(n, b) + k * (CHUNK // 2), CHUNK // 2), CHUNK // 2)]

    def group_start(n, a, b):
        first = (y if n else x) + a + 4
        return chunk_start(n, b) + core * (CHUNK // 2) + lax.rem(first, 4) * GROUP

    def group(n, a, b):
        return kbuf.at[pl.ds(pl.multiple_of(group_start(n, a, b), GROUP), GROUP)]

    def along1(n, step):
        return at(dy=step) if n else at(dx=step)

    def along2(n, step):
        return at(dx=step) if n else at(dy=step)

    def strip(dz):
        place = PLACES[dz % NZ]
        start = group_start(place // 4, 0, 0) + place % 4 * STRIP
        return pl.ds(pl.multiple_of(start, STRIP), STRIP)

    own_rope[...] = jnp.zeros_like(own_rope)
    own_rope[:, :ROPE] = kr[...].astype(jnp.float32).T.astype(jnp.bfloat16)
    mine = pl.ds(pl.multiple_of((2 * y + core) * STRIP, STRIP), STRIP)
    own_slot = (z * NX + x) * 2 + y // 2
    lane = lax.broadcasted_iota(jnp.int32, (STRIP, ROPE + SPANS), 1)
    kbuf[strip(0), :LAT] = lat[mine, :]
    kbuf[strip(0), LAT:] = jnp.where(
        lane == ROPE + own_slot, 1.0, own_rope[mine, :].astype(jnp.float32)
    ).astype(jnp.bfloat16)

    pl.semaphore_wait(barrier, len(peers))

    for d in (6, 7, 1, 2, 4, 5, 3):
        send(kbuf.at[strip(0)], kbuf.at[strip(-d)], pair_of(z_sem, d), at(dz=d))

    tone = 1 - 2 * core
    ahead_z, behind_z = at(dz=tone), at(dz=-tone)

    def wpart(delta, half):
        zz = lax.rem(z + NZ + tone * delta, NZ)
        return wbuf.at[zz, pl.ds(half * (COLS // 2), COLS // 2)]

    def send_w(i, later, half):
        here = wpart(DELTAS[i], half)
        send(here, here, pair_of(o_sem, half, later), ahead_z if DELTAS[later] < 0 else behind_z)

    def wait_w(i, half):
        arrived(wpart(DELTAS[i], half), pair_of(o_sem, half, i), ahead_z if DELTAS[i] > 0 else behind_z)

    def serve_w(i, half):
        wait_w(i, half)
        if i + 2 < NZ:
            send_w(i, i + 2, half)

    loads[0].wait()
    for half in range(2):
        send_w(0, 1, half)
        send_w(0, 2, half)

    square = (SPANS, SPANS)
    places = order[...]
    diagonal = lax.broadcasted_iota(jnp.int32, square, 0) == lax.broadcasted_iota(jnp.int32, square, 1)
    column = jnp.sum(jnp.where(diagonal, jnp.broadcast_to(places, square), 0), axis=1, keepdims=True)
    slot_row = lax.broadcasted_iota(jnp.int32, (SPANS, TOK), 0)
    own_half = lax.broadcasted_iota(jnp.int32, (SPANS, TOK), 1) // SPAN
    own = slot_row == (z * NX + x) * 2 + own_half
    column = jnp.broadcast_to(column, (SPANS, TOK))
    place = jnp.sum(jnp.where(own, column, 0), axis=0, keepdims=True)
    mask = jnp.where(column >= place, HIDDEN, 0.0).astype(jnp.bfloat16)
    for n in (1, 2, 3):
        loads[n].wait()
    rot = qr[...].astype(jnp.float32).T.astype(jnp.bfloat16)
    for h in range(HEADS):
        cols = slice(h * TOK, (h + 1) * TOK)
        qaug[:LAT, cols] = nt_dot(wuk[:, cols], qn[:, cols]).astype(jnp.bfloat16)
        qaug[LAT : LAT + ROPE, cols] = rot[h * ROPE : (h + 1) * ROPE]
        qaug[LAT + ROPE :, cols] = mask

    def hand_on(n, a):
        here = group(n, a, 0)
        if a == 0:
            for s in (1, 3, 2):
                send(here, here, pair_of(w1_sem, n, s), along1(n, s))
        for s in (1, 3):
            send(here, here, pair_of(w2_sem, n, s, a), along2(n, s))

    def from_z(n):
        for d, place in PLACES.items():
            if d and place // 4 == n:
                arrived(kbuf.at[strip(d)], pair_of(z_sem, NZ - d), at(dz=d))
        hand_on(n, 0)

    def first_round(n):
        for a in (1, 3, 2):
            arrived(group(n, a, 0), pair_of(w1_sem, n, 4 - a), along1(n, a))
            hand_on(n, a)
        send(share(core, n, 0), share(core, n, 0), pair_of(p_sem, n, 0), partner)

    def come(n, b):
        for a in (0, 1, 3, 2):
            here = group(n, a, b)
            arrived(here, pair_of(w2_sem, n, 4 - b, a), along2(n, b))
            if (b, a) in ((1, 0), (1, 1), (3, 2), (3, 3)):
                send(here, here, pair_of(w2_sem, n, 2, a), along2(n, -b if b == 1 else 1))
        send(share(core, n, b), share(core, n, b), pair_of(p_sem, n, b), partner)

    def partner_has(n, b):
        arrived(share(other, n, b), pair_of(p_sem, n, b), partner)

    def attend(spots, lo, size, top, total):
        cols = slice(lo, lo + size)
        scores = [nn_dot(kbuf[spot, :], qaug[:, cols]) * FACTOR for spot in spots]
        for spot, score in zip(spots, scores):
            newest = jnp.maximum(top, jnp.max(score, axis=0, keepdims=True))
            shrink = jnp.exp2(top - newest)
            weight = jnp.exp2(score - newest)
            total = total * shrink + jnp.sum(weight.reshape(CHUNK // 8, 8, size), axis=0)
            acc[:, cols] = acc[:, cols] * shrink + tn_dot(kbuf[spot, :LAT], weight.astype(jnp.bfloat16))
            top = newest
        return top, total

    from_z(0)
    first_round(0)
    from_z(1)
    first_round(1)

    row = lax.broadcasted_iota(jnp.int32, (TOK, QUERIES), 0)
    col = lax.rem(lax.broadcasted_iota(jnp.int32, (TOK, QUERIES), 1), TOK)
    seen = (row <= col) & (row >= (col // SPAN) * SPAN)
    score = nn_dot(lat[...], qaug[:LAT, :]) + nn_dot(own_rope[...], qaug[LAT:, :])
    score = jnp.where(seen, score * FACTOR, HIDDEN)
    top = jnp.max(score, axis=0, keepdims=True)
    weight = jnp.exp2(score - top)
    total = jnp.sum(weight.reshape(TOK // 8, 8, QUERIES), axis=0)
    acc[...] = tn_dot(lat[...], weight.astype(jnp.bfloat16))
    loads[4].wait()
    wuv_t[...] = wuv[...].T

    WING = QUERIES // 2
    state = [(top[:, n * WING : (n + 1) * WING], total[:, n * WING : (n + 1) * WING]) for n in range(2)]

    def attend_all(n, b):
        partner_has(n, b)
        spot = chunk(n, b)
        for n in range(2):
            state[n] = attend([spot], n * WING, WING, *state[n])

    def serve(step, half):
        serve_w(2 * step - 1, half)
        serve_w(2 * step, half)

    serve(1, 0)
    attend_all(0, 0)
    come(0, 1)
    come(0, 3)
    attend_all(1, 0)
    come(1, 1)
    come(1, 3)
    serve(1, 1)
    attend_all(0, 1)
    come(0, 2)
    serve(2, 0)
    attend_all(0, 3)
    come(1, 2)
    attend_all(1, 1)
    serve(2, 1)
    attend_all(1, 3)
    attend_all(0, 2)
    serve(3, 0)
    partner_has(1, 2)

    early = list(sent)
    sent.clear()

    for n in range(2):
        half = slice(n * WING, (n + 1) * WING)
        top, total = attend([chunk(1, 2)], n * WING, WING, *state[n])
        whole = jnp.sum(total, axis=0, keepdims=True)
        context = (acc[:, half] / whole).astype(jnp.bfloat16)
        for k in range(HEADS // 2):
            spot = slice((n * HEADS // 2 + k) * VDIM, (n * HEADS // 2 + k + 1) * VDIM)
            hog[x, spot] = nn_dot(wuv_t[spot, :], context[:, k * TOK : (k + 1) * TOK]).astype(jnp.bfloat16)
        for d in (1, 3):
            send(hog.at[x, half], hog.at[x, half], pair_of(a_sem, n, d), at(dx=d))
    serve(3, 1)

    def heads_from(n, o):
        here = hog.at[lax.rem(x + o, NX), n * WING : (n + 1) * WING]
        arrived(here, pair_of(a_sem, n, NX - o), at(dx=o))
        return here

    passed = heads_from(0, 1)
    send(passed, passed, pair_of(a_sem, 0, 2), at(dx=-1))
    passed = heads_from(1, 3)
    send(passed, passed, pair_of(a_sem, 1, 2), at(dx=1))

    tilt = 1 - 2 * lax.rem(z, 2)
    order_y = [lax.rem(z // 2 + NY + step, NY) for step in (0, -tilt, tilt, 2)]
    ahead = []

    def project(*steps):
        right = jnp.concatenate([hog[lax.rem(x + o, NX)] for o in steps], axis=1)
        parts = [(o, slice(i * TOK, (i + 1) * TOK)) for i, o in enumerate(steps)]
        for some in ((0, 1, 2), (3,)) if 0 in steps else (range(NY),):
            if some == (3,):
                for made in early:
                    made.wait_send()
                for half in range(2):
                    wait_w(7, half)
            for n, j in [(n, order_y[n]) for n in some]:
                given = nn_dot(wbuf[2 * j + other], right).astype(jnp.bfloat16)
                for o, part in parts:
                    c1s[o, n] = given[:, part]
                    send(c1s.at[o, n], c1r.at[o, n], pair_of(c1_sem, o, n), partner)
            for n, j in [(n, order_y[n]) for n in some]:
                kept = nn_dot(wbuf[2 * j + core], right)
                for o, part in parts:
                    arrived(c1r.at[o, n], pair_of(c1_sem, o, n), partner)
                    c2s[o, n] = (kept[:, part] + c1r[o, n].astype(jnp.float32)).astype(jnp.bfloat16)
                    sems = (c2_sem.at[0, o, n], c2_sem.at[1, o, y])
                    onward = copy(c2s.at[o, n], c2r.at[o, y], sems, (z, x, j, core))
                    ahead.append((j, onward))

                    @pl.when(j != y)
                    def _():
                        onward.start()

                    @pl.when(j == y)
                    def _():
                        c2r[o, y] = c2s[o, n]

    def collect(o):
        for d in (1, 2, 3):
            yy = lax.rem(y + d, NY)
            arrived(c2r.at[o, yy], (c2_sem.at[0, o, 0], c2_sem.at[1, o, yy]), at(dy=d))
        summed = c2r[o, 0].astype(jnp.float32)
        for k in range(1, NY):
            summed = summed + c2r[o, k].astype(jnp.float32)
        if o:
            c3s[o] = summed.astype(jnp.bfloat16)
            send(c3s.at[o], c3r.at[x], pair_of(c3_sem, o), at(dx=o))
        else:
            c3r[x] = summed.astype(jnp.bfloat16)

    project(0)
    heads_from(1, 1)
    heads_from(0, 3)
    project(1, 3)
    collect(0)
    heads_from(0, 2)
    heads_from(1, 2)
    project(2)
    collect(1)
    collect(3)
    collect(2)
    for d in (1, 2, 3):
        arrived(c3r.at[lax.rem(x + NX - d, NX)], pair_of(c3_sem, d), at(dx=-d))
    out[...] = c3r[...].reshape(NX * COLS, TOK).astype(jnp.float32).T.astype(jnp.bfloat16)

    for j, onward in ahead:

        @pl.when(j != y)
        def _():
            onward.wait_send()

    for made in sent:
        made.wait_send()


def local(q_nope, q_rope, latent, k_rope, span_order, w_uk, w_uv, w_o):
    bf16, f32 = jnp.bfloat16, jnp.float32
    dma = pltpu.SemaphoreType.DMA
    vmem = pl.BlockSpec(memory_space=pltpu.VMEM)
    anywhere = pl.BlockSpec(memory_space=pl.ANY)
    return pl.pallas_call(
        kernel,
        out_shape=jax.ShapeDtypeStruct((TOK, NX * COLS), bf16),
        in_specs=[vmem] * 3 + [anywhere] * 5,
        out_specs=vmem,
        scratch_shapes=[
            pltpu.VMEM((TOK, HEADS * NOPE), bf16),
            pltpu.VMEM((TOK, HEADS * ROPE), bf16),
            pltpu.VMEM((LAT, HEADS * NOPE), bf16),
            pltpu.VMEM((LAT, HEADS * VDIM), bf16),
            pltpu.VMEM((KEYS, WIDE), bf16),
            pltpu.VMEM((TOK, ROPE + SPANS), bf16),
            pltpu.VMEM((WIDE, QUERIES), bf16),
            pltpu.VMEM((LAT, QUERIES), f32),
            pltpu.VMEM((HEADS * VDIM, LAT), bf16),
            pltpu.VMEM((NZ, COLS, HEADS * VDIM), bf16),
            pltpu.VMEM((NX, HEADS * VDIM, TOK), bf16),
            pltpu.VMEM((NX, NY, COLS, TOK), bf16),
            pltpu.VMEM((NX, NY, COLS, TOK), bf16),
            pltpu.VMEM((NX, NY, COLS, TOK), bf16),
            pltpu.VMEM((NX, NY, COLS, TOK), bf16),
            pltpu.VMEM((NX, COLS, TOK), bf16),
            pltpu.VMEM((NX, COLS, TOK), bf16),
            dma((5,)),
            dma((2, NZ)),
            dma((2, 2, 4)),
            dma((2, 2, 4, 4)),
            dma((2, 2, 4)),
            dma((2, 2, NZ)),
            dma((2, 2, NX)),
            dma((2, NX, NY)),
            dma((2, NX, NY)),
            dma((2, NX)),
        ],
        compiler_params=pltpu.CompilerParams(
            collective_id=0, has_side_effects=True, vmem_limit_bytes=56 * 1024 * 1024
        ),
        cost_estimate=pl.CostEstimate(flops=11_000_000_000, bytes_accessed=4_000_000, transcendentals=4_200_000),
    )(latent, k_rope.T, span_order.reshape(1, -1), q_nope, q_rope, w_uk, w_uv, w_o.T)


def solution(mesh):
    torus = Mesh(mesh.devices.reshape(NZ, NX, NY, 2), ("z", "x", "y", "core"))
    ctx, head = ("z", "x"), ("y", "core")
    in_specs = (
        P(ctx, head),
        P(ctx, head),
        P(ctx, None),
        P(ctx, None),
        P(),
        P(None, head),
        P(None, head),
        P(head, ctx),
    )
    return jax.shard_map(local, mesh=torus, in_specs=in_specs, out_specs=P(ctx, head), check_vma=False)
```
